32 devices in a mesh: groups: 2 (over y), dp: 4 (over z), tensor: 2 (over core), section: 2 (over x).
Axes of the slice: x: 2, y: 2, z: 4, core: 2. Of those that a mesh axis runs over, the one named last changes fastest.
Arguments:
- acts: bfloat16 [2, 1024, 8192], P('section', ('groups', 'dp'), 'tensor'), parts along dimension 1, may hold values from -6 to 6
- grads: bfloat16 [2, 1024, 14336], P('section', ('groups', 'dp'), 'tensor'), parts along dimension 1, may hold values from -6 to 6
- proj_in: bfloat16 [2, 64, 8192], P('section', None, 'tensor'), may hold values from -0.0625 to 0.0625
- proj_out: bfloat16 [2, 64, 14336], P('section', None, 'tensor'), may hold values from -0.046875 to 0.046875
- lengths: int32 [8, 32], P(('groups', 'dp')), parts along dimension 0, may hold values from 1 to 64, 128 in all within a row
- query_ids: int32 [8, 32], P(('groups', 'dp')), parts along dimension 0, may hold values from 0 to 31
- train_logged: bfloat16 [2, 1024, 4096], P('section', ('groups', 'dp')), parts along dimension 1, may hold values from -6 to 6
Outputs:
- scores: float32 [128, 1024], P('section', ('groups', 'dp')), parts along dimension 1
The draws below stay inside these ranges and needn't reach their ends.
There are 2 independent parts, one for each index of `groups`. The reference program is written for one: setup_inputs(seed, part) draws one part's arguments, and reference() takes and returns one part's arrays. A program takes and returns all parts, laid end to end along the dimension named above; an argument that names none is the same for every part. Nothing has to cross between parts.
Inputs may be any that keep to these rules, and one draw needn't show every extreme that they name: Each row of lengths sums to 128; in each row the largest is 64.
All inputs are finite; a program needn't handle non-finite values.
Results may differ from the reference program's by a relative error of at most 0.0029.
Values may be sent and summed in bfloat16 or wider, within the bound.
No kernel may reach another device: no remote copies, remote signals or barrier semaphores. Data moves between devices by JAX's collectives and lax.ppermute only.
A program may use at most 64 MiB of HBM per device.

```python
import math
import jax
import jax.numpy as jnp
import numpy as np
from jax import lax

DIN = 8192
DOUT = 14336
RANK = 64
TOK_DEV = 128
EX_DEV = 32
Q_DEV = 32
LAYERS = 2
TOKENS = 512
QUERIES = 128
TRAIN = 512
N_DP = 4


def place_ends(entries, rng, low, top_value):
    spot = [jax.random.randint(jax.random.fold_in(rng, axis), (), 0, length) for axis, length in enumerate(entries.shape)]
    main_axis = entries.shape.index(max(entries.shape))
    neighbour = spot[:main_axis] + [(spot[main_axis] + 1) % entries.shape[main_axis]] + spot[main_axis + 1:]
    return entries.at[tuple(spot)].set(low).at[tuple(neighbour)].set(top_value)


def levels(key, shape, cuts, smallest, high):
    loudness = 1.0
    for position, shards_of in cuts:
        draws = jax.random.uniform(jax.random.fold_in(jax.random.fold_in(key, 6), position), (shards_of,), jnp.float32, smallest / len(cuts), high / len(cuts))
        loudness = loudness * jnp.repeat(jnp.exp(draws), shape[position] // shards_of).reshape((-1,) + (1,) * (len(shape) - 1 - position))
    return loudness


def length_profile(number_of, total, bound, slope):
    loads = [(1 << 20) // math.isqrt(grade ** slope) + 1 for grade in range(2, number_of + 1)]
    spare, holding = total - bound - (number_of - 1), [1] * (number_of - 1)
    while spare > 0:
        free = [i for i in range(number_of - 1) if holding[i] < bound]
        whole, budget = sum([loads[i] for i in free]), spare
        for i in free:
            extra = min(bound - holding[i], max(1, budget * loads[i] // whole), spare)
            holding[i] = holding[i] + extra
            spare = spare - extra
    return np.array([bound] + holding)


def uneven_parts(key, count, total, most, slope):
    if count == 2:
        one = jax.random.randint(key, (), max(1, total - most), min(most, total - 1) + 1)
        return jnp.stack([one, total - one])
    tallies = jnp.asarray(length_profile(count, total, most, slope), jnp.int32)
    pairs = (count - 1) // 2
    source_of, receiver = tallies[1:1 + 2 * pairs:2], tallies[2:2 + 2 * pairs:2]
    room = jnp.minimum(source_of - 1, most - receiver)
    moved = jax.random.randint(jax.random.fold_in(key, 1), (pairs,), 0, 1 << 20) % (room + 1)
    tallies = tallies.at[1:1 + 2 * pairs:2].set(source_of - moved).at[2:2 + 2 * pairs:2].set(receiver + moved)
    return tallies[jax.random.permutation(jax.random.fold_in(key, 2), count)]


def scatter_about(stream_key, dims, scale, limit, split=(), held_as=jnp.bfloat16):
    level = levels(stream_key, dims, split, -0.22, 0.18) if split else 1.0
    array = jax.random.normal(stream_key, dims, jnp.float32) * scale * level
    return jnp.minimum(jnp.maximum(array, -limit), limit).astype(held_as)


def setup_inputs(seed: int = 0, part: int = 0) -> dict:
    splits = jax.random.split(jax.random.key(seed), 8)
    part_splits = jax.random.split(jax.random.fold_in(splits[7], part), 8)
    return {
        "acts": scatter_about(part_splits[0], (LAYERS, TOKENS, DIN), 1.0, 6.0, ((0, 2), (1, 4), (2, 2))),
        "grads": scatter_about(part_splits[1], (LAYERS, TOKENS, DOUT), 1.0, 6.0, ((0, 2), (1, 4), (2, 2))),
        "proj_in": scatter_about(splits[2], (LAYERS, RANK, DIN), DIN ** -0.5, 0.0625, ((0, 2), (2, 2))),
        "proj_out": scatter_about(splits[3], (LAYERS, RANK, DOUT), DOUT ** -0.5, 0.046875, ((0, 2), (2, 2))),
        "lengths": jax.vmap(lambda own: uneven_parts(own, EX_DEV, TOK_DEV, TOK_DEV // 2, 2))(jax.random.split(part_splits[4], N_DP)).reshape((N_DP, EX_DEV)).astype(jnp.int32),
        "query_ids": place_ends(jax.random.randint(part_splits[5], (N_DP, Q_DEV), 0, EX_DEV), jax.random.fold_in(part_splits[5], 1), 0, EX_DEV - 1).astype(jnp.int32),
        "train_logged": scatter_about(part_splits[6], (LAYERS, TRAIN, RANK * RANK), 1.0, 6.0, ((0, 2), (1, 4))),
    }


def reference(acts, grads, proj_in, proj_out, lengths, query_ids, train_logged):
    tok = jnp.arange(TOK_DEV, dtype=jnp.int32)
    ends = jnp.cumsum(lengths, axis=1)
    seg = lax.optimization_barrier(jnp.sum((tok[None, None, :] >= ends[:, :, None]).astype(jnp.int32), axis=1))
    mask = (seg[:, None, :] == query_ids[:, :, None]).astype(jnp.float32)
    weighted = mask / jnp.sqrt(lax.optimization_barrier(jnp.sum(mask, axis=2, keepdims=True)))
    total = jnp.zeros((QUERIES, TRAIN), jnp.float32)
    for layer in range(LAYERS):
        xproj = jnp.dot(acts[layer], proj_in[layer].T, preferred_element_type=jnp.float32).reshape(N_DP, TOK_DEV, RANK)
        gproj = jnp.dot(grads[layer], proj_out[layer].T, preferred_element_type=jnp.float32).reshape(N_DP, TOK_DEV, RANK)
        blocks = jnp.einsum('dqt,dta,dtb->dqab', weighted, gproj, xproj, precision=lax.Precision.HIGHEST)
        blocks = blocks.astype(jnp.bfloat16).reshape(QUERIES, RANK * RANK)
        total = total + jnp.dot(blocks, train_logged[layer].T, preferred_element_type=jnp.float32)
    return total / RANK
```

```python
import functools

import jax
import jax.numpy as jnp
from jax import lax
from jax.experimental import pallas as pl
from jax.experimental.pallas import tpu as pltpu
from jax.sharding import PartitionSpec as P

RANK = 64
LANES = 128
EXTRA = 8
MIB = 1 << 20
NT = (((1,), (1,)), ((), ()))
VMEM = pl.BlockSpec(memory_space=pltpu.VMEM)


def _nt(a, b):
    return lax.dot_general(a, b, NT, preferred_element_type=jnp.float32)


def _cuts(width, parts):
    edges = [width * sum(parts[:i]) // sum(parts) // LANES * LANES for i in range(len(parts))] + [width]
    return list(zip(edges[:-1], edges[1:]))


ACT_PARTS = (1,)
GRAD_PARTS = (7, 5, 2)


def _project_kernel(acts, grads, pin, pout, out, av, gv, piv, pov, sem):
    steps = []
    for big, small, big_v, small_v, parts, row in ((acts, pin, av, piv, ACT_PARTS, RANK), (grads, pout, gv, pov, GRAD_PARTS, 0)):
        for lo, hi in _cuts(big.shape[1], parts):
            cols = pl.ds(lo, hi - lo)
            i = 2 * len(steps)
            pair = (
                pltpu.make_async_copy(small.at[:, cols], small_v.at[:, cols], sem.at[i]),
                pltpu.make_async_copy(big.at[:, cols], big_v.at[:, cols], sem.at[i + 1]),
            )
            for c in pair:
                c.start()
            steps.append((pair, big_v, small_v, cols, row))
    sums = {}
    for pair, big_v, small_v, cols, row in steps:
        for c in pair:
            c.wait()
        part = _nt(small_v[:, cols], big_v[:, cols])
        sums[row] = sums[row] + part if row in sums else part
    for row, value in sums.items():
        out[row : row + RANK, :] = value


def project(acts, grads, pin, pout):
    args = (acts, grads, pin, pout)
    return pl.pallas_call(
        _project_kernel,
        out_shape=jax.ShapeDtypeStruct((2 * RANK, acts.shape[0]), jnp.float32),
        in_specs=[pl.BlockSpec(memory_space=pl.ANY)] * 4,
        out_specs=VMEM,
        scratch_shapes=[pltpu.VMEM(a.shape, a.dtype) for a in args]
        + [pltpu.SemaphoreType.DMA((2 * (len(ACT_PARTS) + len(GRAD_PARTS)),))],
        compiler_params=pltpu.CompilerParams(vmem_limit_bytes=int(53.7 * MIB)),
        name="project",
    )(*args)


def _tags_kernel(lengths, query_ids, out):
    examples, queries, tokens = lengths.shape[1], query_ids.shape[1], out.shape[1]
    length = jnp.broadcast_to(lengths[...].astype(jnp.float32), (examples, examples))
    row = lax.broadcasted_iota(jnp.int32, (examples, examples), 0)
    col = lax.broadcasted_iota(jnp.int32, (examples, examples), 1)
    ends = jnp.sum(jnp.where(col <= row, length, 0.0), axis=1, keepdims=True)
    tok = lax.broadcasted_iota(jnp.int32, (examples, tokens), 1).astype(jnp.float32)
    out[...] = jnp.zeros_like(out)
    out[0:1, :] = jnp.sum(jnp.where(tok >= ends, 1.0, 0.0), axis=0, keepdims=True)
    out[1:2, :queries] = query_ids[...].astype(jnp.float32)


def tags(lengths, query_ids, tokens):
    return pl.pallas_call(
        _tags_kernel,
        out_shape=jax.ShapeDtypeStruct((EXTRA, tokens), jnp.float32),
        in_specs=[VMEM] * 2,
        out_specs=VMEM,
        compiler_params=pltpu.CompilerParams(vmem_limit_bytes=16 * MIB),
        name="tags",
    )(lengths, query_ids)


def _unit(unit, train, queries):
    tokens = unit.shape[1]
    seg = jnp.broadcast_to(unit[2 * RANK : 2 * RANK + 1, :], (queries, tokens))
    ids = jnp.broadcast_to(unit[2 * RANK + 1 : 2 * RANK + 2, :queries], (queries, queries))
    row = lax.broadcasted_iota(jnp.int32, (queries, queries), 0)
    col = lax.broadcasted_iota(jnp.int32, (queries, queries), 1)
    wanted = jnp.sum(jnp.where(row == col, ids, 0.0), axis=1, keepdims=True)
    mask = jnp.where(seg == wanted, 1.0, 0.0)
    scale = 1.0 / jnp.sqrt(jnp.sum(mask, axis=1, keepdims=True))
    mask = mask.astype(jnp.bfloat16)
    g = unit[0:RANK, :]
    x = unit[RANK : 2 * RANK, :]
    g_hi = g.astype(jnp.bfloat16).astype(jnp.float32)
    g_lo = g - g_hi
    x_hi = x.astype(jnp.bfloat16)
    x_lo = (x - x_hi.astype(jnp.float32)).astype(jnp.bfloat16)
    zero = jnp.zeros_like(x_hi)

    def twice(v):
        return jnp.concatenate([jnp.concatenate([v, zero], axis=1), jnp.concatenate([zero, v], axis=1)], axis=0)

    def masked(v):
        rows = []
        for a in range(0, RANK, 2):
            rows.append(
                jnp.concatenate(
                    [jnp.broadcast_to(v[i : i + 1, :], (queries, tokens)).astype(jnp.bfloat16) * mask for i in (a, a + 1)],
                    axis=1,
                )
            )
        return jnp.concatenate(rows, axis=0)

    x_hi, x_lo = twice(x_hi), twice(x_lo)
    left = masked(g_hi)
    blocks = _nt(left, x_hi) + _nt(left, x_lo) + _nt(masked(g_lo), x_hi)
    blocks = jnp.concatenate(
        [(blocks[i * queries : (i + 1) * queries, :] * scale).astype(jnp.bfloat16) for i in range(RANK // 2)], axis=1
    )
    return _nt(blocks, train[...]) * (1.0 / RANK)


def _scores_kernel(queries, step, keep, sections, per, unit, train, *refs):
    out = refs[-1]
    out[...] = refs[0][...] if len(refs) > 1 else jnp.zeros_like(out)
    mine = tuple(step) if isinstance(step, tuple) else (step, step)

    def add(k):
        other = lax.axis_index("dp") ^ k
        row = ((other // per) ^ lax.axis_index("section")) * per + other % per
        out[pl.ds(pl.multiple_of(row * queries, queries), queries), :] = _unit(unit, train, queries)

    core = lax.axis_index("tensor")
    if keep == (True, True):
        add(jnp.where(core == 0, mine[0], mine[1]))
    else:
        c = keep.index(True)
        pl.when(core == c)(lambda: add(mine[c]))


def scores_of(unit, train, queries, step, keep, sections, n_dp, held=None):
    more = () if held is None else (held,)
    return pl.pallas_call(
        functools.partial(_scores_kernel, queries, step, keep, sections, n_dp // sections),
        out_shape=jax.ShapeDtypeStruct((n_dp * queries, train.shape[0]), jnp.float32),
        in_specs=[VMEM] * (2 + len(more)),
        out_specs=VMEM,
        compiler_params=pltpu.CompilerParams(vmem_limit_bytes=16 * MIB),
        name="scores",
    )(unit, train, *more)


def solution(mesh):
    n_dp, cores, sections = mesh.shape["dp"], mesh.shape["tensor"], mesh.shape["section"]

    def swap(v):
        return lax.ppermute(v, "tensor", [(0, 1), (1, 0)])

    def hand(v, steps):
        return lax.ppermute(
            v, ("dp", "tensor"), [(d * cores + t, (d ^ steps[t]) * cores + t) for d in range(n_dp) for t in range(cores)]
        )

    def per_device(acts, grads, proj_in, proj_out, lengths, query_ids, train_logged):
        train, queries = train_logged[0], query_ids.shape[1]
        part = project(acts[0], grads[0], proj_in[0], proj_out[0])
        marks = tags(lengths, query_ids, part.shape[1])
        own = jnp.concatenate([part + swap(part), marks], axis=0)
        rounds = [(2 * j, 2 * j + 1) for j in range(1, n_dp // 2)] + [(1, 1)]
        units = [hand(own, steps) for steps in rounds]
        total = scores_of(own, train, queries, 0, (False, True), sections, n_dp)
        for steps, unit in zip(rounds, units):
            keep = (steps[0] != steps[1], True)
            total = scores_of(unit, train, queries, steps, keep, sections, n_dp, total)
        rows = total.shape[0] // sections
        kept = total[:rows]
        for k in range(1, sections):
            kept = kept + lax.ppermute(total[k * rows : (k + 1) * rows], "section", [(s, s ^ k) for s in range(sections)])
        return kept + swap(kept)

    in_specs = (
        P("section", ("groups", "dp"), "tensor"),
        P("section", ("groups", "dp"), "tensor"),
        P("section", None, "tensor"),
        P("section", None, "tensor"),
        P(("groups", "dp"), None),
        P(("groups", "dp"), None),
        P("section", ("groups", "dp"), None),
    )
    return jax.shard_map(
        per_device, mesh=mesh, in_specs=in_specs, out_specs=P("section", ("groups", "dp")), check_vma=False
    )
```

```python
import functools

import jax
import jax.numpy as jnp
from jax import lax
from jax.experimental import pallas as pl
from jax.experimental.pallas import tpu as pltpu
from jax.sharding import PartitionSpec as P

RANK = 64
LANES = 128
EXTRA = 16
LEVEL = 2.0**16
LEVELS = 7
CHUNK = 8
MIB = 1 << 20
NT = (((1,), (1,)), ((), ()))
VMEM = pl.BlockSpec(memory_space=pltpu.VMEM)


def _nt(a, b):
    return lax.dot_general(a, b, NT, preferred_element_type=jnp.float32)


def _cuts(width, parts):
    edges = [width * sum(parts[:i]) // sum(parts) // LANES * LANES for i in range(len(parts))] + [width]
    return list(zip(edges[:-1], edges[1:]))


ACT_PARTS = (1,)
GRAD_PARTS = (7, 5, 2)


def _project_kernel(acts, grads, pin, pout, out, av, gv, piv, pov, sem):
    steps = []
    for big, small, big_v, small_v, parts, row in ((acts, pin, av, piv, ACT_PARTS, RANK), (grads, pout, gv, pov, GRAD_PARTS, 0)):
        for lo, hi in _cuts(big.shape[1], parts):
            cols = pl.ds(lo, hi - lo)
            i = 2 * len(steps)
            pair = (
                pltpu.make_async_copy(small.at[:, cols], small_v.at[:, cols], sem.at[i]),
                pltpu.make_async_copy(big.at[:, cols], big_v.at[:, cols], sem.at[i + 1]),
            )
            for c in pair:
                c.start()
            steps.append((pair, big_v, small_v, cols, row))
    sums = {}
    for pair, big_v, small_v, cols, row in steps:
        for c in pair:
            c.wait()
        part = _nt(small_v[:, cols], big_v[:, cols])
        sums[row] = sums[row] + part if row in sums else part
    for row, value in sums.items():
        out[row : row + RANK, :] = value


def project(acts, grads, pin, pout):
    args = (acts, grads, pin, pout)
    return pl.pallas_call(
        _project_kernel,
        out_shape=jax.ShapeDtypeStruct((2 * RANK, acts.shape[0]), jnp.float32),
        in_specs=[pl.BlockSpec(memory_space=pl.ANY)] * 4,
        out_specs=VMEM,
        scratch_shapes=[pltpu.VMEM(a.shape, a.dtype) for a in args]
        + [pltpu.SemaphoreType.DMA((2 * (len(ACT_PARTS) + len(GRAD_PARTS)),))],
        compiler_params=pltpu.CompilerParams(vmem_limit_bytes=int(53.7 * MIB)),
        name="project",
    )(*args)


def _tags_kernel(lengths, query_ids, out):
    examples, queries, tokens = lengths.shape[1], query_ids.shape[1], out.shape[1]
    length = jnp.broadcast_to(lengths[...].astype(jnp.float32), (examples, examples))
    row = lax.broadcasted_iota(jnp.int32, (examples, examples), 0)
    col = lax.broadcasted_iota(jnp.int32, (examples, examples), 1)
    ends = jnp.sum(jnp.where(col <= row, length, 0.0), axis=1, keepdims=True)
    tok = lax.broadcasted_iota(jnp.int32, (examples, tokens), 1).astype(jnp.float32)
    out[...] = jnp.zeros_like(out)
    out[0:1, :] = jnp.sum(jnp.where(tok >= ends, 1.0, 0.0), axis=0, keepdims=True)
    out[1:2, :queries] = query_ids[...].astype(jnp.float32)


def tags(lengths, query_ids, tokens):
    return pl.pallas_call(
        _tags_kernel,
        out_shape=jax.ShapeDtypeStruct((EXTRA, tokens), jnp.float32),
        in_specs=[VMEM] * 2,
        out_specs=VMEM,
        compiler_params=pltpu.CompilerParams(vmem_limit_bytes=16 * MIB),
        name="tags",
    )(lengths, query_ids)


def _pack_kernel(mine, other, marks, out):
    out[2 * RANK :, :] = marks[...]
    for i in range(2):
        rows = pl.ds(i * RANK, RANK)
        value = mine[rows, :] + other[rows, :]
        peak = jnp.max(jnp.abs(value), axis=0, keepdims=True)
        scale, level = jnp.ones_like(peak), jnp.zeros_like(peak)
        for _ in range(LEVELS):
            low = peak * scale < 0.5
            scale = jnp.where(low, scale * LEVEL, scale)
            level = jnp.where(low, level + 1.0, level)
        out[rows, :] = value * scale
        out[2 * RANK + 2 + i : 2 * RANK + 3 + i, :] = level


def pack(mine, other, marks):
    return pl.pallas_call(
        _pack_kernel,
        out_shape=jax.ShapeDtypeStruct((2 * RANK + EXTRA, mine.shape[1]), jnp.float32),
        in_specs=[VMEM] * 3,
        out_specs=VMEM,
        compiler_params=pltpu.CompilerParams(vmem_limit_bytes=16 * MIB),
        name="pack",
    )(mine, other, marks)


def _turn_kernel(rows, out):
    out[...] = rows[...].T


def turn(rows):
    return pl.pallas_call(
        _turn_kernel,
        out_shape=jax.ShapeDtypeStruct(rows.shape[::-1], rows.dtype),
        in_specs=[VMEM],
        out_specs=VMEM,
        compiler_params=pltpu.CompilerParams(vmem_limit_bytes=16 * MIB),
        name="turn",
    )(rows)


def _unit(unit, train, queries, first=0, last=RANK):
    tokens = unit.shape[1]
    seg = jnp.broadcast_to(unit[2 * RANK : 2 * RANK + 1, :], (queries, tokens))
    ids = jnp.broadcast_to(unit[2 * RANK + 1 : 2 * RANK + 2, :queries], (queries, queries))
    row = lax.broadcasted_iota(jnp.int32, (queries, queries), 0)
    col = lax.broadcasted_iota(jnp.int32, (queries, queries), 1)
    wanted = jnp.sum(jnp.where(row == col, ids, 0.0), axis=1, keepdims=True)
    mask = jnp.where(seg == wanted, 1.0, 0.0)
    norm = 1.0 / jnp.sqrt(jnp.sum(mask, axis=1, keepdims=True))
    mask = mask.astype(jnp.bfloat16)

    def side(i):
        level = unit[2 * RANK + 2 + i : 2 * RANK + 3 + i, :]
        scale = jnp.ones_like(level)
        for k in range(LEVELS):
            scale = scale * jnp.where(level > k, 1.0 / LEVEL, 1.0)
        value = unit[i * RANK : (i + 1) * RANK, :] * scale
        high = value.astype(jnp.bfloat16).astype(jnp.float32)
        return high, value - high

    def twice(v):
        v = v.astype(jnp.bfloat16)
        zero = jnp.zeros_like(v)
        return jnp.concatenate([jnp.concatenate([v, zero], axis=1), jnp.concatenate([zero, v], axis=1)], axis=0)

    g, x = side(0), side(1)
    right = jnp.concatenate([twice(x[0]), twice(x[1])], axis=0)
    right = jnp.concatenate([right, right], axis=1)
    blocks = []
    for lo in range(first, last, 2 * CHUNK):
        left = []
        for a in range(lo, min(lo + 2 * CHUNK, last), 2):
            parts = [jnp.broadcast_to(v[i : i + 1, :], (queries, tokens)).astype(jnp.bfloat16) * mask for v in g for i in (a, a + 1)]
            left.append(jnp.concatenate(parts, axis=1))
        both = _nt(jnp.concatenate(left, axis=0), right)
        both = both[:, : 2 * RANK] + both[:, 2 * RANK :]
        blocks += [(both[i * queries : (i + 1) * queries, :] * norm).astype(jnp.bfloat16) for i in range(len(left))]
    blocks = jnp.concatenate(blocks, axis=1)
    return jnp.dot(blocks, train[first * RANK : last * RANK, :], preferred_element_type=jnp.float32) * (1.0 / RANK)


def _scores_kernel(queries, step, keep, sections, per, unit, train, *refs):
    out = refs[-1]
    out[...] = refs[0][...] if len(refs) > 1 else jnp.zeros_like(out)
    mine = tuple(step) if isinstance(step, tuple) else (step, step)

    def add(k):
        other = lax.axis_index("dp") ^ k
        row = ((other // per) ^ lax.axis_index("section")) * per + other % per
        out[pl.ds(pl.multiple_of(row * queries, queries), queries), :] = _unit(unit, train, queries)

    core = lax.axis_index("tensor")
    if keep == (True, True):
        add(jnp.where(core == 0, mine[0], mine[1]))
    else:
        c = keep.index(True)
        pl.when(core == c)(lambda: add(mine[c]))


def scores_of(unit, train, queries, step, keep, sections, n_dp, held=None):
    more = () if held is None else (held,)
    return pl.pallas_call(
        functools.partial(_scores_kernel, queries, step, keep, sections, n_dp // sections),
        out_shape=jax.ShapeDtypeStruct((n_dp * queries, train.shape[1]), jnp.float32),
        in_specs=[VMEM] * (2 + len(more)),
        out_specs=VMEM,
        compiler_params=pltpu.CompilerParams(vmem_limit_bytes=16 * MIB),
        name="scores",
    )(unit, train, *more)


def _own_kernel(queries, own, train, out):
    @pl.when(lax.axis_index("tensor") == 0)
    def _():
        out[...] = _unit(own, train, queries)

    @pl.when(lax.axis_index("tensor") != 0)
    def _():
        out[...] = jnp.zeros_like(out)


def _far_kernel(queries, scored, far, train, out):
    sent = lax.axis_index("dp") // 2 == lax.axis_index("section")

    @pl.when(sent)
    def _():
        out[...] = _unit(far, train, queries)

    @pl.when(jnp.logical_not(sent))
    def _():
        out[...] = scored[...]


def _sent_kernel(queries, first, near, train, out):
    sent = lax.axis_index("dp") // 2 == lax.axis_index("section")
    use_near = jnp.logical_not(sent) & (lax.axis_index("tensor") != 0)

    @pl.when(use_near)
    def _():
        out[...] = _unit(near, train, queries)

    @pl.when(jnp.logical_not(use_near))
    def _():
        out[...] = first[...]


def _kept_kernel(queries, scored, far, near, train, out):
    sent = lax.axis_index("dp") // 2 == lax.axis_index("section")
    core = lax.axis_index("tensor")

    @pl.when(jnp.logical_not(sent))
    def _():
        out[...] = _unit(far, train, queries)

    @pl.when(sent & (core == 0))
    def _():
        out[...] = scored[...]

    @pl.when(sent & (core != 0))
    def _():
        out[...] = _unit(near, train, queries)


def _score_call(kernel, queries, name, *args):
    return pl.pallas_call(
        kernel,
        out_shape=jax.ShapeDtypeStruct((queries, args[-1].shape[1]), jnp.float32),
        in_specs=[VMEM] * len(args),
        out_specs=VMEM,
        compiler_params=pltpu.CompilerParams(vmem_limit_bytes=16 * MIB),
        name=name,
    )(*args)


def solution(mesh):
    n_dp, cores, sections = mesh.shape["dp"], mesh.shape["tensor"], mesh.shape["section"]

    def swap(v):
        return lax.ppermute(v, "tensor", [(0, 1), (1, 0)])

    def hand(v, steps):
        return lax.ppermute(
            v,
            ("dp", "tensor"),
            [(d * cores + t, (d ^ steps[1 - t]) * cores + 1 - t) for d in range(n_dp) for t in range(cores)],
        )

    def hand_section(v, step):
        return lax.ppermute(
            v,
            ("tensor", "section"),
            [(t * sections + s, (1 - t) * sections + (s ^ step)) for s in range(sections) for t in range(cores)],
        )

    def four_by_two(own, train, queries):
        far, near = (hand(own, steps).astype(jnp.float32) for steps in ((2, 3), (1, 1)))
        scored = _score_call(functools.partial(_own_kernel, queries), queries, "own", own.astype(jnp.float32), train)
        first = _score_call(functools.partial(_far_kernel, queries), queries, "far", scored, far, train)
        sent = _score_call(functools.partial(_sent_kernel, queries), queries, "sent", first, near, train)
        got = hand_section(sent, 1)
        kept = _score_call(functools.partial(_kept_kernel, queries), queries, "kept", scored, far, near, train)
        kept_first = (lax.axis_index("dp") + lax.axis_index("tensor")) % 2 == 0
        both = jnp.where(kept_first, jnp.concatenate([kept, got]), jnp.concatenate([got, kept]))
        return both + swap(both)

    def per_device(acts, grads, proj_in, proj_out, lengths, query_ids, train_logged):
        train, queries = turn(train_logged[0]), query_ids.shape[1]
        part = project(acts[0], grads[0], proj_in[0], proj_out[0])
        marks = tags(lengths, query_ids, part.shape[1])
        own = pack(part, swap(part), marks).astype(jnp.float16)
        if (n_dp, sections) == (4, 2):
            return four_by_two(own, train, queries)
        rounds = [(2 * j, 2 * j + 1) for j in range(1, n_dp // 2)] + [(1, 1)]
        units = [hand(own, steps) for steps in rounds]
        total = scores_of(own.astype(jnp.float32), train, queries, 0, (False, True), sections, n_dp)
        for steps, unit in zip(rounds, units):
            keep = (steps[0] != steps[1], True)
            total = scores_of(unit.astype(jnp.float32), train, queries, steps, keep, sections, n_dp, total)
        rows = total.shape[0] // sections
        kept = total[:rows]
        for k in range(1, sections):
            kept = kept + hand_section(total[k * rows : (k + 1) * rows], k)
        return kept + swap(kept)

    in_specs = (
        P("section", ("groups", "dp"), "tensor"),
        P("section", ("groups", "dp"), "tensor"),
        P("section", None, "tensor"),
        P("section", None, "tensor"),
        P(("groups", "dp"), None),
        P(("groups", "dp"), None),
        P("section", ("groups", "dp"), None),
    )
    return jax.shard_map(
        per_device, mesh=mesh, in_specs=in_specs, out_specs=P("section", ("groups", "dp")), check_vma=False
    )
```

```python
import functools

import jax
import jax.numpy as jnp
from jax import lax
from jax.experimental import pallas as pl
from jax.experimental.pallas import tpu as pltpu
from jax.sharding import PartitionSpec as P

RANK = 64
LANES = 128
EXTRA = 8
LEVEL = 2.0**16
LEVELS = 7
CHUNK = 8
MIB = 1 << 20
NT = (((1,), (1,)), ((), ()))
VMEM = pl.BlockSpec(memory_space=pltpu.VMEM)


def _nt(a, b):
    return lax.dot_general(a, b, NT, preferred_element_type=jnp.float32)


def _cuts(width, parts):
    edges = [width * sum(parts[:i]) // sum(parts) // LANES * LANES for i in range(len(parts))] + [width]
    return list(zip(edges[:-1], edges[1:]))


ACT_PARTS = (1,)
GRAD_PARTS = (7, 5, 2)


def _project_kernel(acts, grads, pin, pout, out, av, gv, piv, pov, sem):
    steps = []
    for big, small, big_v, small_v, parts, row in ((acts, pin, av, piv, ACT_PARTS, RANK), (grads, pout, gv, pov, GRAD_PARTS, 0)):
        for lo, hi in _cuts(big.shape[1], parts):
            cols = pl.ds(lo, hi - lo)
            i = 2 * len(steps)
            quarter = big.shape[0] // 4
            pair = [pltpu.make_async_copy(small.at[:, cols], small_v.at[:, cols], sem.at[i])]
            for r in range(4):
                rows = pl.ds(r * quarter, quarter)
                pair.append(pltpu.make_async_copy(big.at[rows, cols], big_v.at[rows, cols], sem.at[i + 1]))
            for c in pair:
                c.start()
            steps.append((pair, big_v, small_v, cols, row))
    sums = {}
    for pair, big_v, small_v, cols, row in steps:
        for c in pair:
            c.wait()
        part = _nt(small_v[:, cols], big_v[:, cols])
        sums[row] = sums[row] + part if row in sums else part
    for row, value in sums.items():
        out[row : row + RANK, :] = value


def project(acts, grads, pin, pout):
    args = (acts, grads, pin, pout)
    return pl.pallas_call(
        _project_kernel,
        out_shape=jax.ShapeDtypeStruct((2 * RANK, acts.shape[0]), jnp.float32),
        in_specs=[pl.BlockSpec(memory_space=pl.ANY)] * 4,
        out_specs=VMEM,
        scratch_shapes=[pltpu.VMEM(a.shape, a.dtype) for a in args]
        + [pltpu.SemaphoreType.DMA((2 * (len(ACT_PARTS) + len(GRAD_PARTS)),))],
        compiler_params=pltpu.CompilerParams(vmem_limit_bytes=int(53.7 * MIB)),
        name="project",
    )(*args)


def _tags_kernel(lengths, query_ids, out):
    examples, queries, tokens = lengths.shape[1], query_ids.shape[1], out.shape[1]
    length = jnp.broadcast_to(lengths[...].astype(jnp.float32), (examples, examples))
    row = lax.broadcasted_iota(jnp.int32, (examples, examples), 0)
    col = lax.broadcasted_iota(jnp.int32, (examples, examples), 1)
    ends = jnp.sum(jnp.where(col <= row, length, 0.0), axis=1, keepdims=True)
    tok = lax.broadcasted_iota(jnp.int32, (examples, tokens), 1).astype(jnp.float32)
    out[...] = jnp.zeros_like(out)
    out[0:1, :] = jnp.sum(jnp.where(tok >= ends, 1.0, 0.0), axis=0, keepdims=True)
    out[1:2, :queries] = query_ids[...].astype(jnp.float32)


def tags(lengths, query_ids, tokens):
    return pl.pallas_call(
        _tags_kernel,
        out_shape=jax.ShapeDtypeStruct((EXTRA, tokens), jnp.float32),
        in_specs=[VMEM] * 2,
        out_specs=VMEM,
        compiler_params=pltpu.CompilerParams(vmem_limit_bytes=16 * MIB),
        name="tags",
    )(lengths, query_ids)


def _pack_kernel(mine, other, marks, out):
    out[2 * RANK :, :] = marks[...]
    for i in range(2):
        rows = pl.ds(i * RANK, RANK)
        value = mine[rows, :] + other[rows, :]
        peak = jnp.max(jnp.abs(value), axis=0, keepdims=True)
        scale, level = jnp.ones_like(peak), jnp.zeros_like(peak)
        for _ in range(LEVELS):
            low = peak * scale < 0.5
            scale = jnp.where(low, scale * LEVEL, scale)
            level = jnp.where(low, level + 1.0, level)
        out[rows, :] = value * scale
        out[2 * RANK + 2 + i : 2 * RANK + 3 + i, :] = level


def pack(mine, other, marks):
    return pl.pallas_call(
        _pack_kernel,
        out_shape=jax.ShapeDtypeStruct((2 * RANK + EXTRA, mine.shape[1]), jnp.float32),
        in_specs=[VMEM] * 3,
        out_specs=VMEM,
        compiler_params=pltpu.CompilerParams(vmem_limit_bytes=16 * MIB),
        name="pack",
    )(mine, other, marks)


def _turn_kernel(rows, out):
    out[...] = rows[...].T


def turn(rows):
    return pl.pallas_call(
        _turn_kernel,
        out_shape=jax.ShapeDtypeStruct(rows.shape[::-1], rows.dtype),
        in_specs=[VMEM],
        out_specs=VMEM,
        compiler_params=pltpu.CompilerParams(vmem_limit_bytes=16 * MIB),
        name="turn",
    )(rows)


def _unit(unit, train, queries, first=0, last=RANK):
    tokens = unit.shape[1]
    seg = jnp.broadcast_to(unit[2 * RANK : 2 * RANK + 1, :], (queries, tokens))
    ids = jnp.broadcast_to(unit[2 * RANK + 1 : 2 * RANK + 2, :queries], (queries, queries))
    row = lax.broadcasted_iota(jnp.int32, (queries, queries), 0)
    col = lax.broadcasted_iota(jnp.int32, (queries, queries), 1)
    wanted = jnp.sum(jnp.where(row == col, ids, 0.0), axis=1, keepdims=True)
    mask = jnp.where(seg == wanted, 1.0, 0.0)
    norm = 1.0 / jnp.sqrt(jnp.sum(mask, axis=1, keepdims=True))
    mask = mask.astype(jnp.bfloat16)

    def side(i):
        level = unit[2 * RANK + 2 + i : 2 * RANK + 3 + i, :]
        scale = jnp.ones_like(level)
        for k in range(LEVELS):
            scale = scale * jnp.where(level > k, 1.0 / LEVEL, 1.0)
        value = unit[i * RANK : (i + 1) * RANK, :] * scale
        high = value.astype(jnp.bfloat16).astype(jnp.float32)
        return high, value - high

    def twice(v):
        v = v.astype(jnp.bfloat16)
        zero = jnp.zeros_like(v)
        return jnp.concatenate([jnp.concatenate([v, zero], axis=1), jnp.concatenate([zero, v], axis=1)], axis=0)

    g, x = side(0), side(1)
    right = jnp.concatenate([twice(x[0]), twice(x[1])], axis=0)
    right = jnp.concatenate([right, right], axis=1)
    blocks = []
    for lo in range(first, last, 2 * CHUNK):
        left = []
        for a in range(lo, min(lo + 2 * CHUNK, last), 2):
            parts = [jnp.broadcast_to(v[i : i + 1, :], (queries, tokens)).astype(jnp.bfloat16) * mask for v in g for i in (a, a + 1)]
            left.append(jnp.concatenate(parts, axis=1))
        both = _nt(jnp.concatenate(left, axis=0), right)
        both = both[:, : 2 * RANK] + both[:, 2 * RANK :]
        blocks += [(both[i * queries : (i + 1) * queries, :] * norm).astype(jnp.bfloat16) for i in range(len(left))]
    blocks = jnp.concatenate(blocks, axis=1)
    return jnp.dot(blocks, train[first * RANK : last * RANK, :], preferred_element_type=jnp.float32) * (1.0 / RANK)


def _scores_kernel(queries, step, keep, sections, per, unit, train, *refs):
    out = refs[-1]
    out[...] = refs[0][...] if len(refs) > 1 else jnp.zeros_like(out)
    mine = tuple(step) if isinstance(step, tuple) else (step, step)

    def add(k):
        other = lax.axis_index("dp") ^ k
        row = ((other // per) ^ lax.axis_index("section")) * per + other % per
        out[pl.ds(pl.multiple_of(row * queries, queries), queries), :] = _unit(unit, train, queries)

    core = lax.axis_index("tensor")
    if keep == (True, True):
        add(jnp.where(core == 0, mine[0], mine[1]))
    else:
        c = keep.index(True)
        pl.when(core == c)(lambda: add(mine[c]))


def scores_of(unit, train, queries, step, keep, sections, n_dp, held=None):
    more = () if held is None else (held,)
    return pl.pallas_call(
        functools.partial(_scores_kernel, queries, step, keep, sections, n_dp // sections),
        out_shape=jax.ShapeDtypeStruct((n_dp * queries, train.shape[1]), jnp.float32),
        in_specs=[VMEM] * (2 + len(more)),
        out_specs=VMEM,
        compiler_params=pltpu.CompilerParams(vmem_limit_bytes=16 * MIB),
        name="scores",
    )(unit, train, *more)


def _own_kernel(queries, own, train, out):
    @pl.when(lax.axis_index("tensor") == 0)
    def _():
        out[...] = _unit(own, train, queries)

    @pl.when(lax.axis_index("tensor") != 0)
    def _():
        out[...] = jnp.zeros_like(out)


def _far_kernel(queries, scored, far, train, out):
    sent = lax.axis_index("dp") // 2 == lax.axis_index("section")

    @pl.when(sent)
    def _():
        out[...] = _unit(far, train, queries)

    @pl.when(jnp.logical_not(sent))
    def _():
        out[...] = scored[...]


def _sent_kernel(queries, first, near, train, out):
    sent = lax.axis_index("dp") // 2 == lax.axis_index("section")
    use_near = jnp.logical_not(sent) & (lax.axis_index("tensor") != 0)

    @pl.when(use_near)
    def _():
        out[...] = _unit(near, train, queries)

    @pl.when(jnp.logical_not(use_near))
    def _():
        out[...] = first[...]


def _kept_kernel(queries, scored, far, near, train, out):
    sent = lax.axis_index("dp") // 2 == lax.axis_index("section")
    core = lax.axis_index("tensor")

    @pl.when(jnp.logical_not(sent))
    def _():
        out[...] = _unit(far, train, queries)

    @pl.when(sent & (core == 0))
    def _():
        out[...] = scored[...]

    @pl.when(sent & (core != 0))
    def _():
        out[...] = _unit(near, train, queries)


def _score_call(kernel, queries, name, *args):
    return pl.pallas_call(
        kernel,
        out_shape=jax.ShapeDtypeStruct((queries, args[-1].shape[1]), jnp.float32),
        in_specs=[VMEM] * len(args),
        out_specs=VMEM,
        compiler_params=pltpu.CompilerParams(vmem_limit_bytes=16 * MIB),
        name=name,
    )(*args)


def solution(mesh):
    n_dp, cores, sections = mesh.shape["dp"], mesh.shape["tensor"], mesh.shape["section"]

    def swap(v):
        return lax.ppermute(v, "tensor", [(0, 1), (1, 0)])

    def hand(v, steps):
        return lax.ppermute(
            v,
            ("dp", "tensor"),
            [(d * cores + t, (d ^ steps[1 - t]) * cores + 1 - t) for d in range(n_dp) for t in range(cores)],
        )

    def hand_section(v, step):
        return lax.ppermute(
            v,
            ("tensor", "section"),
            [(t * sections + s, (1 - t) * sections + (s ^ step)) for s in range(sections) for t in range(cores)],
        )

    def four_by_two(own, train, queries):
        far, near = (hand(own, steps).astype(jnp.float32) for steps in ((2, 3), (1, 1)))
        scored = _score_call(functools.partial(_own_kernel, queries), queries, "own", own.astype(jnp.float32), train)
        first = _score_call(functools.partial(_far_kernel, queries), queries, "far", scored, far, train)
        sent = _score_call(functools.partial(_sent_kernel, queries), queries, "sent", first, near, train)
        got = hand_section(sent.astype(jnp.bfloat16), 1).astype(jnp.float32)
        kept = _score_call(functools.partial(_kept_kernel, queries), queries, "kept", scored, far, near, train)
        kept_first = (lax.axis_index("dp") + lax.axis_index("tensor")) % 2 == 0
        both = jnp.where(kept_first, jnp.concatenate([kept, got]), jnp.concatenate([got, kept]))
        return both + swap(both)

    def per_device(acts, grads, proj_in, proj_out, lengths, query_ids, train_logged):
        train, queries = turn(train_logged[0]), query_ids.shape[1]
        part = project(acts[0], grads[0], proj_in[0], proj_out[0])
        marks = tags(lengths, query_ids, part.shape[1])
        own = pack(part, swap(part), marks).astype(jnp.float16)
        if (n_dp, sections) == (4, 2):
            return four_by_two(own, train, queries)
        rounds = [(2 * j, 2 * j + 1) for j in range(1, n_dp // 2)] + [(1, 1)]
        units = [hand(own, steps) for steps in rounds]
        total = scores_of(own.astype(jnp.float32), train, queries, 0, (False, True), sections, n_dp)
        for steps, unit in zip(rounds, units):
            keep = (steps[0] != steps[1], True)
            total = scores_of(unit.astype(jnp.float32), train, queries, steps, keep, sections, n_dp, total)
        rows = total.shape[0] // sections
        kept = total[:rows]
        for k in range(1, sections):
            kept = kept + hand_section(total[k * rows : (k + 1) * rows], k)
        return kept + swap(kept)

    in_specs = (
        P("section", ("groups", "dp"), "tensor"),
        P("section", ("groups", "dp"), "tensor"),
        P("section", None, "tensor"),
        P("section", None, "tensor"),
        P(("groups", "dp"), None),
        P(("groups", "dp"), None),
        P("section", ("groups", "dp"), None),
    )
    return jax.shard_map(
        per_device, mesh=mesh, in_specs=in_specs, out_specs=P("section", ("groups", "dp")), check_vma=False
    )
```

```python
import functools

import jax
import jax.numpy as jnp
from jax import lax
from jax.experimental import pallas as pl
from jax.experimental.pallas import tpu as pltpu
from jax.sharding import PartitionSpec as P

RANK = 64
LANES = 128
EXTRA = 8
LEVEL = 2.0**16
LEVELS = 7
CHUNK = 8
MIB = 1 << 20
NT = (((1,), (1,)), ((), ()))
VMEM = pl.BlockSpec(memory_space=pltpu.VMEM)


def _nt(a, b):
    return lax.dot_general(a, b, NT, preferred_element_type=jnp.float32)


def _cuts(width, parts):
    edges = [width * sum(parts[:i]) // sum(parts) // LANES * LANES for i in range(len(parts))] + [width]
    return list(zip(edges[:-1], edges[1:]))


ACT_PARTS = (1,)
GRAD_PARTS = (7, 5, 2)


def _project_kernel(acts, grads, pin, pout, out, av, gv, piv, pov, sem):
    steps = []
    for big, small, big_v, small_v, parts, row in ((acts, pin, av, piv, ACT_PARTS, RANK), (grads, pout, gv, pov, GRAD_PARTS, 0)):
        for lo, hi in _cuts(big.shape[1], parts):
            cols = pl.ds(lo, hi - lo)
            i = 2 * len(steps)
            quarter = big.shape[0] // 4
            pair = [pltpu.make_async_copy(small.at[:, cols], small_v.at[:, cols], sem.at[i])]
            for r in range(4):
                rows = pl.ds(r * quarter, quarter)
                pair.append(pltpu.make_async_copy(big.at[rows, cols], big_v.at[rows, cols], sem.at[i + 1]))
            for c in pair:
                c.start()
            steps.append((pair, big_v, small_v, cols, row))
    sums = {}
    for pair, big_v, small_v, cols, row in steps:
        for c in pair:
            c.wait()
        part = _nt(small_v[:, cols], big_v[:, cols])
        sums[row] = sums[row] + part if row in sums else part
    for row, value in sums.items():
        out[row : row + RANK, :] = value


def project(acts, grads, pin, pout):
    args = (acts, grads, pin, pout)
    return pl.pallas_call(
        _project_kernel,
        out_shape=jax.ShapeDtypeStruct((2 * RANK, acts.shape[0]), jnp.float32),
        in_specs=[pl.BlockSpec(memory_space=pl.ANY)] * 4,
        out_specs=VMEM,
        scratch_shapes=[pltpu.VMEM(a.shape, a.dtype) for a in args]
        + [pltpu.SemaphoreType.DMA((2 * (len(ACT_PARTS) + len(GRAD_PARTS)),))],
        compiler_params=pltpu.CompilerParams(vmem_limit_bytes=int(53.7 * MIB)),
        name="project",
    )(*args)


def _tags_kernel(lengths, query_ids, out):
    examples, queries, tokens = lengths.shape[1], query_ids.shape[1], out.shape[1]
    length = jnp.broadcast_to(lengths[...].astype(jnp.float32), (examples, examples))
    row = lax.broadcasted_iota(jnp.int32, (examples, examples), 0)
    col = lax.broadcasted_iota(jnp.int32, (examples, examples), 1)
    ends = jnp.sum(jnp.where(col <= row, length, 0.0), axis=1, keepdims=True)
    tok = lax.broadcasted_iota(jnp.int32, (examples, tokens), 1).astype(jnp.float32)
    out[...] = jnp.zeros_like(out)
    out[0:1, :] = jnp.sum(jnp.where(tok >= ends, 1.0, 0.0), axis=0, keepdims=True)
    out[1:2, :queries] = query_ids[...].astype(jnp.float32)


def tags(lengths, query_ids, tokens):
    return pl.pallas_call(
        _tags_kernel,
        out_shape=jax.ShapeDtypeStruct((EXTRA, tokens), jnp.float32),
        in_specs=[VMEM] * 2,
        out_specs=VMEM,
        compiler_params=pltpu.CompilerParams(vmem_limit_bytes=16 * MIB),
        name="tags",
    )(lengths, query_ids)


def _pack_kernel(mine, other, marks, out):
    out[2 * RANK :, :] = marks[...]
    for i in range(2):
        rows = pl.ds(i * RANK, RANK)
        value = mine[rows, :] + other[rows, :]
        peak = jnp.max(jnp.abs(value), axis=0, keepdims=True)
        scale, level = jnp.ones_like(peak), jnp.zeros_like(peak)
        for _ in range(LEVELS):
            low = peak * scale < 0.5
            scale = jnp.where(low, scale * LEVEL, scale)
            level = jnp.where(low, level + 1.0, level)
        out[rows, :] = value * scale
        out[2 * RANK + 2 + i : 2 * RANK + 3 + i, :] = level


def pack(mine, other, marks):
    return pl.pallas_call(
        _pack_kernel,
        out_shape=jax.ShapeDtypeStruct((2 * RANK + EXTRA, mine.shape[1]), jnp.float32),
        in_specs=[VMEM] * 3,
        out_specs=VMEM,
        compiler_params=pltpu.CompilerParams(vmem_limit_bytes=16 * MIB),
        name="pack",
    )(mine, other, marks)


def _turn_kernel(rows, out):
    out[...] = rows[...].T


def turn(rows):
    return pl.pallas_call(
        _turn_kernel,
        out_shape=jax.ShapeDtypeStruct(rows.shape[::-1], rows.dtype),
        in_specs=[VMEM],
        out_specs=VMEM,
        compiler_params=pltpu.CompilerParams(vmem_limit_bytes=16 * MIB),
        name="turn",
    )(rows)


def _unit(unit, train, queries, first=0, last=RANK):
    tokens = unit.shape[1]
    seg = jnp.broadcast_to(unit[2 * RANK : 2 * RANK + 1, :], (queries, tokens))
    ids = jnp.broadcast_to(unit[2 * RANK + 1 : 2 * RANK + 2, :queries], (queries, queries))
    row = lax.broadcasted_iota(jnp.int32, (queries, queries), 0)
    col = lax.broadcasted_iota(jnp.int32, (queries, queries), 1)
    wanted = jnp.sum(jnp.where(row == col, ids, 0.0), axis=1, keepdims=True)
    mask = jnp.where(seg == wanted, 1.0, 0.0)
    norm = 1.0 / jnp.sqrt(jnp.sum(mask, axis=1, keepdims=True))
    mask = mask.astype(jnp.bfloat16)

    def side(i):
        level = unit[2 * RANK + 2 + i : 2 * RANK + 3 + i, :]
        scale = jnp.ones_like(level)
        for k in range(LEVELS):
            scale = scale * jnp.where(level > k, 1.0 / LEVEL, 1.0)
        value = unit[i * RANK : (i + 1) * RANK, :] * scale
        high = value.astype(jnp.bfloat16).astype(jnp.float32)
        return high, value - high

    def twice(v):
        v = v.astype(jnp.bfloat16)
        zero = jnp.zeros_like(v)
        return jnp.concatenate([jnp.concatenate([v, zero], axis=1), jnp.concatenate([zero, v], axis=1)], axis=0)

    g, x = side(0), side(1)
    right = jnp.concatenate([twice(x[0]), twice(x[1])], axis=0)
    right = jnp.concatenate([right, right], axis=1)
    blocks = []
    for lo in range(first, last, 2 * CHUNK):
        left = []
        for a in range(lo, min(lo + 2 * CHUNK, last), 2):
            parts = [jnp.broadcast_to(v[i : i + 1, :], (queries, tokens)).astype(jnp.bfloat16) * mask for v in g for i in (a, a + 1)]
            left.append(jnp.concatenate(parts, axis=1))
        both = _nt(jnp.concatenate(left, axis=0), right)
        both = both[:, : 2 * RANK] + both[:, 2 * RANK :]
        blocks += [(both[i * queries : (i + 1) * queries, :] * norm).astype(jnp.bfloat16) for i in range(len(left))]
    blocks = jnp.concatenate(blocks, axis=1)
    return jnp.dot(blocks, train[first * RANK : last * RANK, :], preferred_element_type=jnp.float32) * (1.0 / RANK)


def _scores_kernel(queries, step, keep, sections, per, unit, train, *refs):
    out = refs[-1]
    out[...] = refs[0][...] if len(refs) > 1 else jnp.zeros_like(out)
    mine = tuple(step) if isinstance(step, tuple) else (step, step)

    def add(k):
        other = lax.axis_index("dp") ^ k
        row = ((other // per) ^ lax.axis_index("section")) * per + other % per
        out[pl.ds(pl.multiple_of(row * queries, queries), queries), :] = _unit(unit, train, queries)

    core = lax.axis_index("tensor")
    if keep == (True, True):
        add(jnp.where(core == 0, mine[0], mine[1]))
    else:
        c = keep.index(True)
        pl.when(core == c)(lambda: add(mine[c]))


def scores_of(unit, train, queries, step, keep, sections, n_dp, held=None):
    more = () if held is None else (held,)
    return pl.pallas_call(
        functools.partial(_scores_kernel, queries, step, keep, sections, n_dp // sections),
        out_shape=jax.ShapeDtypeStruct((n_dp * queries, train.shape[1]), jnp.float32),
        in_specs=[VMEM] * (2 + len(more)),
        out_specs=VMEM,
        compiler_params=pltpu.CompilerParams(vmem_limit_bytes=16 * MIB),
        name="scores",
    )(unit, train, *more)


def _own_kernel(queries, own, train, out):
    @pl.when(lax.axis_index("tensor") == 0)
    def _():
        out[...] = _unit(own, train, queries)

    @pl.when(lax.axis_index("tensor") != 0)
    def _():
        out[...] = jnp.zeros_like(out)


def _far_kernel(queries, scored, far, train, out):
    sent = lax.axis_index("dp") // 2 == lax.axis_index("section")

    @pl.when(sent)
    def _():
        out[...] = _unit(far, train, queries)

    @pl.when(jnp.logical_not(sent))
    def _():
        out[...] = scored[...]


def _sent_kernel(queries, first, near, train, out):
    sent = lax.axis_index("dp") // 2 == lax.axis_index("section")
    use_near = jnp.logical_not(sent) & (lax.axis_index("tensor") != 0)

    @pl.when(use_near)
    def _():
        out[...] = _unit(near, train, queries)

    @pl.when(jnp.logical_not(use_near))
    def _():
        out[...] = first[...]


def _kept_kernel(queries, scored, far, near, train, out):
    sent = lax.axis_index("dp") // 2 == lax.axis_index("section")
    core = lax.axis_index("tensor")

    @pl.when(jnp.logical_not(sent))
    def _():
        out[...] = _unit(far, train, queries)

    @pl.when(sent & (core == 0))
    def _():
        out[...] = scored[...]

    @pl.when(sent & (core != 0))
    def _():
        out[...] = _unit(near, train, queries)


def _score_call(kernel, queries, name, *args):
    return pl.pallas_call(
        kernel,
        out_shape=jax.ShapeDtypeStruct((queries, args[-1].shape[1]), jnp.float32),
        in_specs=[VMEM] * len(args),
        out_specs=VMEM,
        compiler_params=pltpu.CompilerParams(vmem_limit_bytes=16 * MIB),
        name=name,
    )(*args)


def solution(mesh):
    n_dp, cores, sections = mesh.shape["dp"], mesh.shape["tensor"], mesh.shape["section"]

    def swap(v):
        return lax.ppermute(v, "tensor", [(0, 1), (1, 0)])

    def hand(v, steps):
        return lax.ppermute(
            v,
            ("dp", "tensor"),
            [(d * cores + t, (d ^ steps[1 - t]) * cores + 1 - t) for d in range(n_dp) for t in range(cores)],
        )

    def hand_section(v, step):
        return lax.ppermute(
            v,
            ("tensor", "section"),
            [(t * sections + s, (1 - t) * sections + (s ^ step)) for s in range(sections) for t in range(cores)],
        )

    def four_by_two(own, train, queries):
        far = hand(own, (2, 3)).astype(jnp.float32)
        pairs = [pair for d in range(n_dp) for pair in ((d * cores, (d ^ 1) * cores + 1), (d * cores + 1, d * cores))]
        near = lax.ppermute(own, ("dp", "tensor"), pairs).astype(jnp.float32)
        scored = _score_call(functools.partial(_own_kernel, queries), queries, "own", own.astype(jnp.float32), train)
        first = _score_call(functools.partial(_far_kernel, queries), queries, "far", scored, far, train)
        sent = _score_call(functools.partial(_sent_kernel, queries), queries, "sent", first, near, train)
        got = hand_section(sent.astype(jnp.bfloat16), 1).astype(jnp.float32)
        kept = _score_call(functools.partial(_kept_kernel, queries), queries, "kept", scored, far, near, train)
        kept_first = (lax.axis_index("dp") + lax.axis_index("tensor")) % 2 == 0
        both = jnp.where(kept_first, jnp.concatenate([kept, got]), jnp.concatenate([got, kept]))
        return both + swap(both)

    def per_device(acts, grads, proj_in, proj_out, lengths, query_ids, train_logged):
        train, queries = turn(train_logged[0]), query_ids.shape[1]
        part = project(acts[0], grads[0], proj_in[0], proj_out[0])
        marks = tags(lengths, query_ids, part.shape[1])
        own = pack(part, swap(part), marks).astype(jnp.float16)
        if (n_dp, sections) == (4, 2):
            return four_by_two(own, train, queries)
        rounds = [(2 * j, 2 * j + 1) for j in range(1, n_dp // 2)] + [(1, 1)]
        units = [hand(own, steps) for steps in rounds]
        total = scores_of(own.astype(jnp.float32), train, queries, 0, (False, True), sections, n_dp)
        for steps, unit in zip(rounds, units):
            keep = (steps[0] != steps[1], True)
            total = scores_of(unit.astype(jnp.float32), train, queries, steps, keep, sections, n_dp, total)
        rows = total.shape[0] // sections
        kept = total[:rows]
        for k in range(1, sections):
            kept = kept + hand_section(total[k * rows : (k + 1) * rows], k)
        return kept + swap(kept)

    in_specs = (
        P("section", ("groups", "dp"), "tensor"),
        P("section", ("groups", "dp"), "tensor"),
        P("section", None, "tensor"),
        P("section", None, "tensor"),
        P(("groups", "dp"), None),
        P(("groups", "dp"), None),
        P("section", ("groups", "dp"), None),
    )
    return jax.shard_map(
        per_device, mesh=mesh, in_specs=in_specs, out_specs=P("section", ("groups", "dp")), check_vma=False
    )
```

```python
import functools

import jax
import jax.numpy as jnp
from jax import lax
from jax.experimental import pallas as pl
from jax.experimental.pallas import tpu as pltpu
from jax.sharding import PartitionSpec as P

RANK = 64
LANES = 128
EXTRA = 8
LEVEL = 2.0**16
LEVELS = 7
CHUNK = 8
MIB = 1 << 20
NT = (((1,), (1,)), ((), ()))
VMEM = pl.BlockSpec(memory_space=pltpu.VMEM)


def _nt(a, b):
    return lax.dot_general(a, b, NT, preferred_element_type=jnp.float32)


def _cuts(width, parts):
    edges = [width * sum(parts[:i]) // sum(parts) // LANES * LANES for i in range(len(parts))] + [width]
    return list(zip(edges[:-1], edges[1:]))


ACT_PARTS = (1,)
GRAD_PARTS = (7, 5, 2)


def _project_kernel(acts, grads, pin, pout, out, av, gv, piv, pov, sem):
    steps = []
    for big, small, big_v, small_v, parts, row in ((acts, pin, av, piv, ACT_PARTS, RANK), (grads, pout, gv, pov, GRAD_PARTS, 0)):
        for lo, hi in _cuts(big.shape[1], parts):
            cols = pl.ds(lo, hi - lo)
            i = 2 * len(steps)
            quarter = big.shape[0] // 4
            pair = [pltpu.make_async_copy(small.at[:, cols], small_v.at[:, cols], sem.at[i])]
            for r in range(4):
                rows = pl.ds(r * quarter, quarter)
                pair.append(pltpu.make_async_copy(big.at[rows, cols], big_v.at[rows, cols], sem.at[i + 1]))
            for c in pair:
                c.start()
            steps.append((pair, big_v, small_v, cols, row))
    sums = {}
    for pair, big_v, small_v, cols, row in steps:
        for c in pair:
            c.wait()
        part = _nt(small_v[:, cols], big_v[:, cols])
        sums[row] = sums[row] + part if row in sums else part
    for row, value in sums.items():
        out[row : row + RANK, :] = value


def project(acts, grads, pin, pout):
    args = (acts, grads, pin, pout)
    return pl.pallas_call(
        _project_kernel,
        out_shape=jax.ShapeDtypeStruct((2 * RANK, acts.shape[0]), jnp.float32),
        in_specs=[pl.BlockSpec(memory_space=pl.ANY)] * 4,
        out_specs=VMEM,
        scratch_shapes=[pltpu.VMEM(a.shape, a.dtype) for a in args]
        + [pltpu.SemaphoreType.DMA((2 * (len(ACT_PARTS) + len(GRAD_PARTS)),))],
        compiler_params=pltpu.CompilerParams(vmem_limit_bytes=int(53.7 * MIB)),
        name="project",
    )(*args)


def _tags_kernel(lengths, query_ids, out):
    examples, queries, tokens = lengths.shape[1], query_ids.shape[1], out.shape[1]
    length = jnp.broadcast_to(lengths[...].astype(jnp.float32), (examples, examples))
    row = lax.broadcasted_iota(jnp.int32, (examples, examples), 0)
    col = lax.broadcasted_iota(jnp.int32, (examples, examples), 1)
    ends = jnp.sum(jnp.where(col <= row, length, 0.0), axis=1, keepdims=True)
    tok = lax.broadcasted_iota(jnp.int32, (examples, tokens), 1).astype(jnp.float32)
    out[...] = jnp.zeros_like(out)
    out[0:1, :] = jnp.sum(jnp.where(tok >= ends, 1.0, 0.0), axis=0, keepdims=True)
    out[1:2, :queries] = query_ids[...].astype(jnp.float32)


def tags(lengths, query_ids, tokens):
    return pl.pallas_call(
        _tags_kernel,
        out_shape=jax.ShapeDtypeStruct((EXTRA, tokens), jnp.float32),
        in_specs=[VMEM] * 2,
        out_specs=VMEM,
        compiler_params=pltpu.CompilerParams(vmem_limit_bytes=16 * MIB),
        name="tags",
    )(lengths, query_ids)


def _pack_kernel(mine, other, marks, out):
    out[2 * RANK :, :] = marks[...]
    for i in range(2):
        rows = pl.ds(i * RANK, RANK)
        value = mine[rows, :] + other[rows, :]
        peak = jnp.max(jnp.abs(value), axis=0, keepdims=True)
        scale, level = jnp.ones_like(peak), jnp.zeros_like(peak)
        for _ in range(LEVELS):
            low = peak * scale < 0.5
            scale = jnp.where(low, scale * LEVEL, scale)
            level = jnp.where(low, level + 1.0, level)
        out[rows, :] = value * scale
        out[2 * RANK + 2 + i : 2 * RANK + 3 + i, :] = level


def pack(mine, other, marks):
    return pl.pallas_call(
        _pack_kernel,
        out_shape=jax.ShapeDtypeStruct((2 * RANK + EXTRA, mine.shape[1]), jnp.float32),
        in_specs=[VMEM] * 3,
        out_specs=VMEM,
        compiler_params=pltpu.CompilerParams(vmem_limit_bytes=16 * MIB),
        name="pack",
    )(mine, other, marks)


def _turn_kernel(rows, out):
    out[...] = rows[...].T


def turn(rows):
    return pl.pallas_call(
        _turn_kernel,
        out_shape=jax.ShapeDtypeStruct(rows.shape[::-1], rows.dtype),
        in_specs=[VMEM],
        out_specs=VMEM,
        compiler_params=pltpu.CompilerParams(vmem_limit_bytes=16 * MIB),
        name="turn",
    )(rows)


def _unit(unit, train, queries, first=0, last=RANK):
    tokens = unit.shape[1]
    seg = jnp.broadcast_to(unit[2 * RANK : 2 * RANK + 1, :], (queries, tokens))
    ids = jnp.broadcast_to(unit[2 * RANK + 1 : 2 * RANK + 2, :queries], (queries, queries))
    row = lax.broadcasted_iota(jnp.int32, (queries, queries), 0)
    col = lax.broadcasted_iota(jnp.int32, (queries, queries), 1)
    wanted = jnp.sum(jnp.where(row == col, ids, 0.0), axis=1, keepdims=True)
    mask = jnp.where(seg == wanted, 1.0, 0.0)
    norm = 1.0 / jnp.sqrt(jnp.sum(mask, axis=1, keepdims=True))
    mask = mask.astype(jnp.bfloat16)

    def side(i):
        level = unit[2 * RANK + 2 + i : 2 * RANK + 3 + i, :]
        scale = jnp.ones_like(level)
        for k in range(LEVELS):
            scale = scale * jnp.where(level > k, 1.0 / LEVEL, 1.0)
        value = unit[i * RANK : (i + 1) * RANK, :] * scale
        high = value.astype(jnp.bfloat16).astype(jnp.float32)
        return high, value - high

    def twice(v):
        v = v.astype(jnp.bfloat16)
        zero = jnp.zeros_like(v)
        return jnp.concatenate([jnp.concatenate([v, zero], axis=1), jnp.concatenate([zero, v], axis=1)], axis=0)

    g, x = side(0), side(1)
    right = jnp.concatenate([twice(x[0]), twice(x[1])], axis=0)
    right = jnp.concatenate([right, right], axis=1)
    blocks = []
    for lo in range(first, last, 2 * CHUNK):
        left = []
        for a in range(lo, min(lo + 2 * CHUNK, last), 2):
            parts = [jnp.broadcast_to(v[i : i + 1, :], (queries, tokens)).astype(jnp.bfloat16) * mask for v in g for i in (a, a + 1)]
            left.append(jnp.concatenate(parts, axis=1))
        both = _nt(jnp.concatenate(left, axis=0), right)
        both = both[:, : 2 * RANK] + both[:, 2 * RANK :]
        blocks += [(both[i * queries : (i + 1) * queries, :] * norm).astype(jnp.bfloat16) for i in range(len(left))]
    blocks = jnp.concatenate(blocks, axis=1)
    return jnp.dot(blocks, train[first * RANK : last * RANK, :], preferred_element_type=jnp.float32) * (1.0 / RANK)


def _scores_kernel(queries, step, keep, sections, per, unit, train, *refs):
    out = refs[-1]
    out[...] = refs[0][...] if len(refs) > 1 else jnp.zeros_like(out)
    mine = tuple(step) if isinstance(step, tuple) else (step, step)

    def add(k):
        other = lax.axis_index("dp") ^ k
        row = ((other // per) ^ lax.axis_index("section")) * per + other % per
        out[pl.ds(pl.multiple_of(row * queries, queries), queries), :] = _unit(unit, train, queries)

    core = lax.axis_index("tensor")
    if keep == (True, True):
        add(jnp.where(core == 0, mine[0], mine[1]))
    else:
        c = keep.index(True)
        pl.when(core == c)(lambda: add(mine[c]))


def scores_of(unit, train, queries, step, keep, sections, n_dp, held=None):
    more = () if held is None else (held,)
    return pl.pallas_call(
        functools.partial(_scores_kernel, queries, step, keep, sections, n_dp // sections),
        out_shape=jax.ShapeDtypeStruct((n_dp * queries, train.shape[1]), jnp.float32),
        in_specs=[VMEM] * (2 + len(more)),
        out_specs=VMEM,
        compiler_params=pltpu.CompilerParams(vmem_limit_bytes=16 * MIB),
        name="scores",
    )(unit, train, *more)


def _own_kernel(queries, own, train, out):
    @pl.when(lax.axis_index("tensor") == 0)
    def _():
        out[...] = _unit(own, train, queries)

    @pl.when(lax.axis_index("tensor") != 0)
    def _():
        out[...] = jnp.zeros_like(out)


def _far_kernel(queries, scored, far, train, out):
    sent = lax.axis_index("dp") // 2 == lax.axis_index("section")

    @pl.when(sent)
    def _():
        out[...] = _unit(far, train, queries)

    @pl.when(jnp.logical_not(sent))
    def _():
        out[...] = scored[...]


def _sent_kernel(queries, first, near, train, out):
    sent = lax.axis_index("dp") // 2 == lax.axis_index("section")
    use_near = jnp.logical_not(sent) & (lax.axis_index("tensor") != 0)

    @pl.when(use_near)
    def _():
        out[...] = _unit(near, train, queries)

    @pl.when(jnp.logical_not(use_near))
    def _():
        out[...] = first[...]


def _kept_kernel(queries, scored, far, near, train, out):
    sent = lax.axis_index("dp") // 2 == lax.axis_index("section")
    core = lax.axis_index("tensor")

    @pl.when(jnp.logical_not(sent))
    def _():
        out[...] = _unit(far, train, queries)

    @pl.when(sent & (core == 0))
    def _():
        out[...] = scored[...]

    @pl.when(sent & (core != 0))
    def _():
        out[...] = _unit(near, train, queries)


def _score_call(kernel, queries, name, *args):
    return pl.pallas_call(
        kernel,
        out_shape=jax.ShapeDtypeStruct((queries, args[-1].shape[1]), jnp.float32),
        in_specs=[VMEM] * len(args),
        out_specs=VMEM,
        compiler_params=pltpu.CompilerParams(vmem_limit_bytes=16 * MIB),
        name=name,
    )(*args)


def solution(mesh):
    n_dp, cores, sections = mesh.shape["dp"], mesh.shape["tensor"], mesh.shape["section"]

    def swap(v):
        return lax.ppermute(v, "tensor", [(0, 1), (1, 0)])

    def hand(v, steps):
        return lax.ppermute(
            v,
            ("dp", "tensor"),
            [(d * cores + t, (d ^ steps[1 - t]) * cores + 1 - t) for d in range(n_dp) for t in range(cores)],
        )

    def hand_section(v, step):
        return lax.ppermute(
            v,
            ("tensor", "section"),
            [(t * sections + s, (1 - t) * sections + (s ^ step)) for s in range(sections) for t in range(cores)],
        )

    def four_by_two(own, train, queries):
        far = hand(own, (2, 3)).astype(jnp.float32)
        pairs = [pair for d in range(n_dp) for pair in ((d * cores, (d ^ 1) * cores + 1), (d * cores + 1, d * cores))]
        near = lax.ppermute(own, ("dp", "tensor"), pairs).astype(jnp.float32)
        scored = _score_call(functools.partial(_own_kernel, queries), queries, "own", own.astype(jnp.float32), train)
        first = _score_call(functools.partial(_far_kernel, queries), queries, "far", scored, far, train)
        sent = _score_call(functools.partial(_sent_kernel, queries), queries, "sent", first, near, train)
        got = hand_section(sent, 1)
        kept = _score_call(functools.partial(_kept_kernel, queries), queries, "kept", scored, far, near, train)
        kept_first = (lax.axis_index("dp") + lax.axis_index("tensor")) % 2 == 0
        both = jnp.where(kept_first, jnp.concatenate([kept, got]), jnp.concatenate([got, kept]))
        return both + swap(both)

    def per_device(acts, grads, proj_in, proj_out, lengths, query_ids, train_logged):
        train, queries = turn(train_logged[0]), query_ids.shape[1]
        part = project(acts[0], grads[0], proj_in[0], proj_out[0])
        marks = tags(lengths, query_ids, part.shape[1])
        own = pack(part, swap(part), marks).astype(jnp.float16)
        if (n_dp, sections) == (4, 2):
            return four_by_two(own, train, queries)
        rounds = [(2 * j, 2 * j + 1) for j in range(1, n_dp // 2)] + [(1, 1)]
        units = [hand(own, steps) for steps in rounds]
        total = scores_of(own.astype(jnp.float32), train, queries, 0, (False, True), sections, n_dp)
        for steps, unit in zip(rounds, units):
            keep = (steps[0] != steps[1], True)
            total = scores_of(unit.astype(jnp.float32), train, queries, steps, keep, sections, n_dp, total)
        rows = total.shape[0] // sections
        kept = total[:rows]
        for k in range(1, sections):
            kept = kept + hand_section(total[k * rows : (k + 1) * rows], k)
        return kept + swap(kept)

    in_specs = (
        P("section", ("groups", "dp"), "tensor"),
        P("section", ("groups", "dp"), "tensor"),
        P("section", None, "tensor"),
        P("section", None, "tensor"),
        P(("groups", "dp"), None),
        P(("groups", "dp"), None),
        P("section", ("groups", "dp"), None),
    )
    return jax.shard_map(
        per_device, mesh=mesh, in_specs=in_specs, out_specs=P("section", ("groups", "dp")), check_vma=False
    )
```

```python
import functools

import jax
import jax.numpy as jnp
from jax import lax
from jax.experimental import pallas as pl
from jax.experimental.pallas import tpu as pltpu
from jax.sharding import PartitionSpec as P

RANK = 64
LANES = 128
EXTRA = 8
LEVEL = 2.0**16
LEVELS = 7
CHUNK = 8
MIB = 1 << 20
NT = (((1,), (1,)), ((), ()))
VMEM = pl.BlockSpec(memory_space=pltpu.VMEM)


def _nt(a, b):
    return lax.dot_general(a, b, NT, preferred_element_type=jnp.float32)


def _cuts(width, parts):
    edges = [width * sum(parts[:i]) // sum(parts) // LANES * LANES for i in range(len(parts))] + [width]
    return list(zip(edges[:-1], edges[1:]))


ACT_PARTS = (1,)
GRAD_PARTS = (7, 5, 2)


def _project_kernel(acts, grads, pin, pout, out, av, gv, piv, pov, sem):
    steps = []
    for big, small, big_v, small_v, parts, row in ((acts, pin, av, piv, ACT_PARTS, RANK), (grads, pout, gv, pov, GRAD_PARTS, 0)):
        for lo, hi in _cuts(big.shape[1], parts):
            cols = pl.ds(lo, hi - lo)
            i = 2 * len(steps)
            quarter = big.shape[0] // 4
            pair = [pltpu.make_async_copy(small.at[:, cols], small_v.at[:, cols], sem.at[i])]
            for r in range(4):
                rows = pl.ds(r * quarter, quarter)
                pair.append(pltpu.make_async_copy(big.at[rows, cols], big_v.at[rows, cols], sem.at[i + 1]))
            for c in pair:
                c.start()
            steps.append((pair, big_v, small_v, cols, row))
    sums = {}
    for pair, big_v, small_v, cols, row in steps:
        for c in pair:
            c.wait()
        part = _nt(small_v[:, cols], big_v[:, cols])
        sums[row] = sums[row] + part if row in sums else part
    for row, value in sums.items():
        out[row : row + RANK, :] = value


def project(acts, grads, pin, pout):
    args = (acts, grads, pin, pout)
    return pl.pallas_call(
        _project_kernel,
        out_shape=jax.ShapeDtypeStruct((2 * RANK, acts.shape[0]), jnp.float32),
        in_specs=[pl.BlockSpec(memory_space=pl.ANY)] * 4,
        out_specs=VMEM,
        scratch_shapes=[pltpu.VMEM(a.shape, a.dtype) for a in args]
        + [pltpu.SemaphoreType.DMA((2 * (len(ACT_PARTS) + len(GRAD_PARTS)),))],
        compiler_params=pltpu.CompilerParams(vmem_limit_bytes=int(53.7 * MIB)),
        name="project",
    )(*args)


def _tags_kernel(lengths, query_ids, out):
    examples, queries, tokens = lengths.shape[1], query_ids.shape[1], out.shape[1]
    length = jnp.broadcast_to(lengths[...].astype(jnp.float32), (examples, examples))
    row = lax.broadcasted_iota(jnp.int32, (examples, examples), 0)
    col = lax.broadcasted_iota(jnp.int32, (examples, examples), 1)
    ends = jnp.sum(jnp.where(col <= row, length, 0.0), axis=1, keepdims=True)
    tok = lax.broadcasted_iota(jnp.int32, (examples, tokens), 1).astype(jnp.float32)
    out[...] = jnp.zeros_like(out)
    out[0:1, :] = jnp.sum(jnp.where(tok >= ends, 1.0, 0.0), axis=0, keepdims=True)
    out[1:2, :queries] = query_ids[...].astype(jnp.float32)


def tags(lengths, query_ids, tokens):
    return pl.pallas_call(
        _tags_kernel,
        out_shape=jax.ShapeDtypeStruct((EXTRA, tokens), jnp.float32),
        in_specs=[VMEM] * 2,
        out_specs=VMEM,
        compiler_params=pltpu.CompilerParams(vmem_limit_bytes=16 * MIB),
        name="tags",
    )(lengths, query_ids)


def _pack_kernel(mine, other, marks, out):
    out[2 * RANK :, :] = marks[...]
    for i in range(2):
        rows = pl.ds(i * RANK, RANK)
        value = mine[rows, :] + other[rows, :]
        peak = jnp.max(jnp.abs(value), axis=0, keepdims=True)
        scale, level = jnp.ones_like(peak), jnp.zeros_like(peak)
        for _ in range(LEVELS):
            low = peak * scale < 0.5
            scale = jnp.where(low, scale * LEVEL, scale)
            level = jnp.where(low, level + 1.0, level)
        out[rows, :] = value * scale
        out[2 * RANK + 2 + i : 2 * RANK + 3 + i, :] = level


def pack(mine, other, marks):
    return pl.pallas_call(
        _pack_kernel,
        out_shape=jax.ShapeDtypeStruct((2 * RANK + EXTRA, mine.shape[1]), jnp.float32),
        in_specs=[VMEM] * 3,
        out_specs=VMEM,
        compiler_params=pltpu.CompilerParams(vmem_limit_bytes=16 * MIB),
        name="pack",
    )(mine, other, marks)


def _turn_kernel(rows, out):
    out[...] = rows[...].T


def turn(rows):
    return pl.pallas_call(
        _turn_kernel,
        out_shape=jax.ShapeDtypeStruct(rows.shape[::-1], rows.dtype),
        in_specs=[VMEM],
        out_specs=VMEM,
        compiler_params=pltpu.CompilerParams(vmem_limit_bytes=16 * MIB),
        name="turn",
    )(rows)


def _unit(unit, train, queries, first=0, last=RANK):
    tokens = unit.shape[1]
    seg = jnp.broadcast_to(unit[2 * RANK : 2 * RANK + 1, :], (queries, tokens))
    ids = jnp.broadcast_to(unit[2 * RANK + 1 : 2 * RANK + 2, :queries], (queries, queries))
    row = lax.broadcasted_iota(jnp.int32, (queries, queries), 0)
    col = lax.broadcasted_iota(jnp.int32, (queries, queries), 1)
    wanted = jnp.sum(jnp.where(row == col, ids, 0.0), axis=1, keepdims=True)
    mask = jnp.where(seg == wanted, 1.0, 0.0)
    norm = 1.0 / jnp.sqrt(jnp.sum(mask, axis=1, keepdims=True))
    mask = mask.astype(jnp.bfloat16)

    def side(i):
        level = unit[2 * RANK + 2 + i : 2 * RANK + 3 + i, :]
        scale = jnp.ones_like(level)
        for k in range(LEVELS):
            scale = scale * jnp.where(level > k, 1.0 / LEVEL, 1.0)
        value = unit[i * RANK : (i + 1) * RANK, :] * scale
        high = value.astype(jnp.bfloat16).astype(jnp.float32)
        return high, value - high

    def twice(v):
        v = v.astype(jnp.bfloat16)
        zero = jnp.zeros_like(v)
        return jnp.concatenate([jnp.concatenate([v, zero], axis=1), jnp.concatenate([zero, v], axis=1)], axis=0)

    g, x = side(0), side(1)
    right = jnp.concatenate([twice(x[0]), twice(x[1])], axis=0)
    right = jnp.concatenate([right, right], axis=1)
    blocks = []
    for lo in range(first, last, 2 * CHUNK):
        left = []
        for a in range(lo, min(lo + 2 * CHUNK, last), 2):
            parts = [jnp.broadcast_to(v[i : i + 1, :], (queries, tokens)).astype(jnp.bfloat16) * mask for v in g for i in (a, a + 1)]
            left.append(jnp.concatenate(parts, axis=1))
        both = _nt(jnp.concatenate(left, axis=0), right)
        both = both[:, : 2 * RANK] + both[:, 2 * RANK :]
        blocks += [(both[i * queries : (i + 1) * queries, :] * norm).astype(jnp.bfloat16) for i in range(len(left))]
    blocks = jnp.concatenate(blocks, axis=1)
    return jnp.dot(blocks, train[first * RANK : last * RANK, :], preferred_element_type=jnp.float32) * (1.0 / RANK)


def _scores_kernel(queries, step, keep, sections, per, unit, train, *refs):
    out = refs[-1]
    out[...] = refs[0][...] if len(refs) > 1 else jnp.zeros_like(out)
    mine = tuple(step) if isinstance(step, tuple) else (step, step)

    def add(k):
        other = lax.axis_index("dp") ^ k
        row = ((other // per) ^ lax.axis_index("section")) * per + other % per
        out[pl.ds(pl.multiple_of(row * queries, queries), queries), :] = _unit(unit, train, queries)

    core = lax.axis_index("tensor")
    if keep == (True, True):
        add(jnp.where(core == 0, mine[0], mine[1]))
    else:
        c = keep.index(True)
        pl.when(core == c)(lambda: add(mine[c]))


def scores_of(unit, train, queries, step, keep, sections, n_dp, held=None):
    more = () if held is None else (held,)
    return pl.pallas_call(
        functools.partial(_scores_kernel, queries, step, keep, sections, n_dp // sections),
        out_shape=jax.ShapeDtypeStruct((n_dp * queries, train.shape[1]), jnp.float32),
        in_specs=[VMEM] * (2 + len(more)),
        out_specs=VMEM,
        compiler_params=pltpu.CompilerParams(vmem_limit_bytes=16 * MIB),
        name="scores",
    )(unit, train, *more)


def _own_kernel(queries, own, train, out):
    @pl.when(lax.axis_index("tensor") == 1)
    def _():
        out[...] = _unit(own, train, queries)

    @pl.when(lax.axis_index("tensor") != 1)
    def _():
        out[...] = jnp.zeros_like(out)


def _far_kernel(queries, scored, far, train, out):
    sent = lax.axis_index("dp") // 2 == lax.axis_index("section")

    @pl.when(sent)
    def _():
        out[...] = _unit(far, train, queries)

    @pl.when(jnp.logical_not(sent))
    def _():
        out[...] = scored[...]


def _sent_kernel(queries, first, near, train, out):
    sent = lax.axis_index("dp") // 2 == lax.axis_index("section")
    use_near = jnp.logical_not(sent) & (lax.axis_index("tensor") != 1)

    @pl.when(use_near)
    def _():
        out[...] = _unit(near, train, queries)

    @pl.when(jnp.logical_not(use_near))
    def _():
        out[...] = first[...]


def _kept_kernel(queries, scored, far, near, train, out):
    sent = lax.axis_index("dp") // 2 == lax.axis_index("section")
    core = lax.axis_index("tensor")

    @pl.when(jnp.logical_not(sent))
    def _():
        out[...] = _unit(far, train, queries)

    @pl.when(sent & (core == 1))
    def _():
        out[...] = scored[...]

    @pl.when(sent & (core != 1))
    def _():
        out[...] = _unit(near, train, queries)


def _score_call(kernel, queries, name, *args):
    return pl.pallas_call(
        kernel,
        out_shape=jax.ShapeDtypeStruct((queries, args[-1].shape[1]), jnp.float32),
        in_specs=[VMEM] * len(args),
        out_specs=VMEM,
        compiler_params=pltpu.CompilerParams(vmem_limit_bytes=16 * MIB),
        name=name,
    )(*args)


def solution(mesh):
    n_dp, cores, sections = mesh.shape["dp"], mesh.shape["tensor"], mesh.shape["section"]

    def swap(v):
        return lax.ppermute(v, "tensor", [(0, 1), (1, 0)])

    def hand(v, steps):
        return lax.ppermute(
            v,
            ("dp", "tensor"),
            [(d * cores + t, (d ^ steps[1 - t]) * cores + 1 - t) for d in range(n_dp) for t in range(cores)],
        )

    def hand_section(v, step):
        return lax.ppermute(
            v,
            ("tensor", "section"),
            [(t * sections + s, (1 - t) * sections + (s ^ step)) for s in range(sections) for t in range(cores)],
        )

    def four_by_two(own, train, queries):
        far = hand(own, (3, 2)).astype(jnp.float32)
        pairs = [pair for d in range(n_dp) for pair in ((d * cores + 1, (d ^ 1) * cores), (d * cores, d * cores + 1))]
        near = lax.ppermute(own, ("dp", "tensor"), pairs).astype(jnp.float32)
        scored = _score_call(functools.partial(_own_kernel, queries), queries, "own", own.astype(jnp.float32), train)
        first = _score_call(functools.partial(_far_kernel, queries), queries, "far", scored, far, train)
        sent = _score_call(functools.partial(_sent_kernel, queries), queries, "sent", first, near, train)
        got = hand_section(sent, 1)
        kept = _score_call(functools.partial(_kept_kernel, queries), queries, "kept", scored, far, near, train)
        kept_first = (lax.axis_index("dp") + lax.axis_index("tensor")) % 2 == 1
        both = jnp.where(kept_first, jnp.concatenate([kept, got]), jnp.concatenate([got, kept]))
        return both + swap(both)

    def per_device(acts, grads, proj_in, proj_out, lengths, query_ids, train_logged):
        train, queries = turn(train_logged[0]), query_ids.shape[1]
        part = project(acts[0], grads[0], proj_in[0], proj_out[0])
        marks = tags(lengths, query_ids, part.shape[1])
        own = pack(part, swap(part), marks).astype(jnp.float16)
        if (n_dp, sections) == (4, 2):
            return four_by_two(own, train, queries)
        rounds = [(2 * j, 2 * j + 1) for j in range(1, n_dp // 2)] + [(1, 1)]
        units = [hand(own, steps) for steps in rounds]
        total = scores_of(own.astype(jnp.float32), train, queries, 0, (False, True), sections, n_dp)
        for steps, unit in zip(rounds, units):
            keep = (steps[0] != steps[1], True)
            total = scores_of(unit.astype(jnp.float32), train, queries, steps, keep, sections, n_dp, total)
        rows = total.shape[0] // sections
        kept = total[:rows]
        for k in range(1, sections):
            kept = kept + hand_section(total[k * rows : (k + 1) * rows], k)
        return kept + swap(kept)

    in_specs = (
        P("section", ("groups", "dp"), "tensor"),
        P("section", ("groups", "dp"), "tensor"),
        P("section", None, "tensor"),
        P("section", None, "tensor"),
        P(("groups", "dp"), None),
        P(("groups", "dp"), None),
        P("section", ("groups", "dp"), None),
    )
    return jax.shard_map(
        per_device, mesh=mesh, in_specs=in_specs, out_specs=P("section", ("groups", "dp")), check_vma=False
    )
```

```python
import functools

import jax
import jax.numpy as jnp
from jax import lax
from jax.experimental import pallas as pl
from jax.experimental.pallas import tpu as pltpu
from jax.sharding import PartitionSpec as P

RANK = 64
LANES = 128
EXTRA = 8
LEVEL = 2.0**16
LEVELS = 7
CHUNK = 8
MIB = 1 << 20
NT = (((1,), (1,)), ((), ()))
VMEM = pl.BlockSpec(memory_space=pltpu.VMEM)


def _nt(a, b):
    return lax.dot_general(a, b, NT, preferred_element_type=jnp.float32)


def _cuts(width, parts):
    edges = [width * sum(parts[:i]) // sum(parts) // LANES * LANES for i in range(len(parts))] + [width]
    return list(zip(edges[:-1], edges[1:]))


ACT_PARTS = (1,)
GRAD_PARTS = (7, 6, 1)


def _project_kernel(acts, grads, pin, pout, out, av, gv, piv, pov, sem):
    steps = []
    for big, small, big_v, small_v, parts, row in ((acts, pin, av, piv, ACT_PARTS, RANK), (grads, pout, gv, pov, GRAD_PARTS, 0)):
        for lo, hi in _cuts(big.shape[1], parts):
            cols = pl.ds(lo, hi - lo)
            i = 2 * len(steps)
            quarter = big.shape[0] // 4
            pair = [pltpu.make_async_copy(small.at[:, cols], small_v.at[:, cols], sem.at[i])]
            for r in range(4):
                rows = pl.ds(r * quarter, quarter)
                pair.append(pltpu.make_async_copy(big.at[rows, cols], big_v.at[rows, cols], sem.at[i + 1]))
            for c in pair:
                c.start()
            steps.append((pair, big_v, small_v, cols, row))
    sums = {}
    for pair, big_v, small_v, cols, row in steps:
        for c in pair:
            c.wait()
        part = _nt(small_v[:, cols], big_v[:, cols])
        sums[row] = sums[row] + part if row in sums else part
    for row, value in sums.items():
        out[row : row + RANK, :] = value


def project(acts, grads, pin, pout):
    args = (acts, grads, pin, pout)
    return pl.pallas_call(
        _project_kernel,
        out_shape=jax.ShapeDtypeStruct((2 * RANK, acts.shape[0]), jnp.float32),
        in_specs=[pl.BlockSpec(memory_space=pl.ANY)] * 4,
        out_specs=VMEM,
        scratch_shapes=[pltpu.VMEM(a.shape, a.dtype) for a in args]
        + [pltpu.SemaphoreType.DMA((2 * (len(ACT_PARTS) + len(GRAD_PARTS)),))],
        compiler_params=pltpu.CompilerParams(vmem_limit_bytes=int(53.7 * MIB)),
        name="project",
    )(*args)


def _tags_kernel(lengths, query_ids, out):
    examples, queries, tokens = lengths.shape[1], query_ids.shape[1], out.shape[1]
    length = jnp.broadcast_to(lengths[...].astype(jnp.float32), (examples, examples))
    row = lax.broadcasted_iota(jnp.int32, (examples, examples), 0)
    col = lax.broadcasted_iota(jnp.int32, (examples, examples), 1)
    ends = jnp.sum(jnp.where(col <= row, length, 0.0), axis=1, keepdims=True)
    tok = lax.broadcasted_iota(jnp.int32, (examples, tokens), 1).astype(jnp.float32)
    out[...] = jnp.zeros_like(out)
    out[0:1, :] = jnp.sum(jnp.where(tok >= ends, 1.0, 0.0), axis=0, keepdims=True)
    out[1:2, :queries] = query_ids[...].astype(jnp.float32)


def tags(lengths, query_ids, tokens):
    return pl.pallas_call(
        _tags_kernel,
        out_shape=jax.ShapeDtypeStruct((EXTRA, tokens), jnp.float32),
        in_specs=[VMEM] * 2,
        out_specs=VMEM,
        compiler_params=pltpu.CompilerParams(vmem_limit_bytes=16 * MIB),
        name="tags",
    )(lengths, query_ids)


def _pack_kernel(mine, other, marks, out):
    out[2 * RANK :, :] = marks[...]
    for i in range(2):
        rows = pl.ds(i * RANK, RANK)
        value = mine[rows, :] + other[rows, :]
        peak = jnp.max(jnp.abs(value), axis=0, keepdims=True)
        scale, level = jnp.ones_like(peak), jnp.zeros_like(peak)
        for _ in range(LEVELS):
            low = peak * scale < 0.5
            scale = jnp.where(low, scale * LEVEL, scale)
            level = jnp.where(low, level + 1.0, level)
        out[rows, :] = value * scale
        out[2 * RANK + 2 + i : 2 * RANK + 3 + i, :] = level


def pack(mine, other, marks):
    return pl.pallas_call(
        _pack_kernel,
        out_shape=jax.ShapeDtypeStruct((2 * RANK + EXTRA, mine.shape[1]), jnp.float32),
        in_specs=[VMEM] * 3,
        out_specs=VMEM,
        compiler_params=pltpu.CompilerParams(vmem_limit_bytes=16 * MIB),
        name="pack",
    )(mine, other, marks)


def _turn_kernel(rows, out):
    out[...] = rows[...].T


def turn(rows):
    return pl.pallas_call(
        _turn_kernel,
        out_shape=jax.ShapeDtypeStruct(rows.shape[::-1], rows.dtype),
        in_specs=[VMEM],
        out_specs=VMEM,
        compiler_params=pltpu.CompilerParams(vmem_limit_bytes=16 * MIB),
        name="turn",
    )(rows)


def _unit(unit, train, queries, first=0, last=RANK):
    tokens = unit.shape[1]
    seg = jnp.broadcast_to(unit[2 * RANK : 2 * RANK + 1, :], (queries, tokens))
    ids = jnp.broadcast_to(unit[2 * RANK + 1 : 2 * RANK + 2, :queries], (queries, queries))
    row = lax.broadcasted_iota(jnp.int32, (queries, queries), 0)
    col = lax.broadcasted_iota(jnp.int32, (queries, queries), 1)
    wanted = jnp.sum(jnp.where(row == col, ids, 0.0), axis=1, keepdims=True)
    mask = jnp.where(seg == wanted, 1.0, 0.0)
    norm = 1.0 / jnp.sqrt(jnp.sum(mask, axis=1, keepdims=True))
    mask = mask.astype(jnp.bfloat16)

    def side(i):
        level = unit[2 * RANK + 2 + i : 2 * RANK + 3 + i, :]
        scale = jnp.ones_like(level)
        for k in range(LEVELS):
            scale = scale * jnp.where(level > k, 1.0 / LEVEL, 1.0)
        value = unit[i * RANK : (i + 1) * RANK, :] * scale
        high = value.astype(jnp.bfloat16).astype(jnp.float32)
        return high, value - high

    def twice(v):
        v = v.astype(jnp.bfloat16)
        zero = jnp.zeros_like(v)
        return jnp.concatenate([jnp.concatenate([v, zero], axis=1), jnp.concatenate([zero, v], axis=1)], axis=0)

    g, x = side(0), side(1)
    right = jnp.concatenate([twice(x[0]), twice(x[1])], axis=0)
    right = jnp.concatenate([right, right], axis=1)
    blocks = []
    for lo in range(first, last, 2 * CHUNK):
        left = []
        for a in range(lo, min(lo + 2 * CHUNK, last), 2):
            parts = [jnp.broadcast_to(v[i : i + 1, :], (queries, tokens)).astype(jnp.bfloat16) * mask for v in g for i in (a, a + 1)]
            left.append(jnp.concatenate(parts, axis=1))
        both = _nt(jnp.concatenate(left, axis=0), right)
        both = both[:, : 2 * RANK] + both[:, 2 * RANK :]
        blocks += [(both[i * queries : (i + 1) * queries, :] * norm).astype(jnp.bfloat16) for i in range(len(left))]
    blocks = jnp.concatenate(blocks, axis=1)
    return jnp.dot(blocks, train[first * RANK : last * RANK, :], preferred_element_type=jnp.float32) * (1.0 / RANK)


def _scores_kernel(queries, step, keep, sections, per, unit, train, *refs):
    out = refs[-1]
    out[...] = refs[0][...] if len(refs) > 1 else jnp.zeros_like(out)
    mine = tuple(step) if isinstance(step, tuple) else (step, step)

    def add(k):
        other = lax.axis_index("dp") ^ k
        row = ((other // per) ^ lax.axis_index("section")) * per + other % per
        out[pl.ds(pl.multiple_of(row * queries, queries), queries), :] = _unit(unit, train, queries)

    core = lax.axis_index("tensor")
    if keep == (True, True):
        add(jnp.where(core == 0, mine[0], mine[1]))
    else:
        c = keep.index(True)
        pl.when(core == c)(lambda: add(mine[c]))


def scores_of(unit, train, queries, step, keep, sections, n_dp, held=None):
    more = () if held is None else (held,)
    return pl.pallas_call(
        functools.partial(_scores_kernel, queries, step, keep, sections, n_dp // sections),
        out_shape=jax.ShapeDtypeStruct((n_dp * queries, train.shape[1]), jnp.float32),
        in_specs=[VMEM] * (2 + len(more)),
        out_specs=VMEM,
        compiler_params=pltpu.CompilerParams(vmem_limit_bytes=16 * MIB),
        name="scores",
    )(unit, train, *more)


def _own_kernel(queries, own, train, out):
    @pl.when(lax.axis_index("tensor") == 1)
    def _():
        out[...] = _unit(own, train, queries)

    @pl.when(lax.axis_index("tensor") != 1)
    def _():
        out[...] = jnp.zeros_like(out)


def _far_kernel(queries, scored, far, train, out):
    sent = lax.axis_index("dp") // 2 == lax.axis_index("section")

    @pl.when(sent)
    def _():
        out[...] = _unit(far, train, queries)

    @pl.when(jnp.logical_not(sent))
    def _():
        out[...] = scored[...]


def _sent_kernel(queries, first, near, train, out):
    sent = lax.axis_index("dp") // 2 == lax.axis_index("section")
    use_near = jnp.logical_not(sent) & (lax.axis_index("tensor") != 1)

    @pl.when(use_near)
    def _():
        out[...] = _unit(near, train, queries)

    @pl.when(jnp.logical_not(use_near))
    def _():
        out[...] = first[...]


def _kept_kernel(queries, scored, far, near, train, out):
    sent = lax.axis_index("dp") // 2 == lax.axis_index("section")
    core = lax.axis_index("tensor")

    @pl.when(jnp.logical_not(sent))
    def _():
        out[...] = _unit(far, train, queries)

    @pl.when(sent & (core == 1))
    def _():
        out[...] = scored[...]

    @pl.when(sent & (core != 1))
    def _():
        out[...] = _unit(near, train, queries)


def _score_call(kernel, queries, name, *args):
    return pl.pallas_call(
        kernel,
        out_shape=jax.ShapeDtypeStruct((queries, args[-1].shape[1]), jnp.float32),
        in_specs=[VMEM] * len(args),
        out_specs=VMEM,
        compiler_params=pltpu.CompilerParams(vmem_limit_bytes=16 * MIB),
        name=name,
    )(*args)


def solution(mesh):
    n_dp, cores, sections = mesh.shape["dp"], mesh.shape["tensor"], mesh.shape["section"]

    def swap(v):
        return lax.ppermute(v, "tensor", [(0, 1), (1, 0)])

    def hand(v, steps):
        return lax.ppermute(
            v,
            ("dp", "tensor"),
            [(d * cores + t, (d ^ steps[1 - t]) * cores + 1 - t) for d in range(n_dp) for t in range(cores)],
        )

    def hand_section(v, step):
        return lax.ppermute(
            v,
            ("tensor", "section"),
            [(t * sections + s, (1 - t) * sections + (s ^ step)) for s in range(sections) for t in range(cores)],
        )

    def four_by_two(own, train, queries):
        far = hand(own, (3, 2)).astype(jnp.float32)
        pairs = [pair for d in range(n_dp) for pair in ((d * cores + 1, (d ^ 1) * cores), (d * cores, d * cores + 1))]
        near = lax.ppermute(own, ("dp", "tensor"), pairs).astype(jnp.float32)
        scored = _score_call(functools.partial(_own_kernel, queries), queries, "own", own.astype(jnp.float32), train)
        first = _score_call(functools.partial(_far_kernel, queries), queries, "far", scored, far, train)
        sent = _score_call(functools.partial(_sent_kernel, queries), queries, "sent", first, near, train)
        got = hand_section(sent, 1)
        kept = _score_call(functools.partial(_kept_kernel, queries), queries, "kept", scored, far, near, train)
        kept_first = (lax.axis_index("dp") + lax.axis_index("tensor")) % 2 == 1
        both = jnp.where(kept_first, jnp.concatenate([kept, got]), jnp.concatenate([got, kept]))
        return both + swap(both)

    def per_device(acts, grads, proj_in, proj_out, lengths, query_ids, train_logged):
        train, queries = turn(train_logged[0]), query_ids.shape[1]
        part = project(acts[0], grads[0], proj_in[0], proj_out[0])
        marks = tags(lengths, query_ids, part.shape[1])
        own = pack(part, swap(part), marks).astype(jnp.float16)
        if (n_dp, sections) == (4, 2):
            return four_by_two(own, train, queries)
        rounds = [(2 * j, 2 * j + 1) for j in range(1, n_dp // 2)] + [(1, 1)]
        units = [hand(own, steps) for steps in rounds]
        total = scores_of(own.astype(jnp.float32), train, queries, 0, (False, True), sections, n_dp)
        for steps, unit in zip(rounds, units):
            keep = (steps[0] != steps[1], True)
            total = scores_of(unit.astype(jnp.float32), train, queries, steps, keep, sections, n_dp, total)
        rows = total.shape[0] // sections
        kept = total[:rows]
        for k in range(1, sections):
            kept = kept + hand_section(total[k * rows : (k + 1) * rows], k)
        return kept + swap(kept)

    in_specs = (
        P("section", ("groups", "dp"), "tensor"),
        P("section", ("groups", "dp"), "tensor"),
        P("section", None, "tensor"),
        P("section", None, "tensor"),
        P(("groups", "dp"), None),
        P(("groups", "dp"), None),
        P("section", ("groups", "dp"), None),
    )
    return jax.shard_map(
        per_device, mesh=mesh, in_specs=in_specs, out_specs=P("section", ("groups", "dp")), check_vma=False
    )
```
